512 devices in a mesh: blk: 16 (over y, x_lo), cluster: 32 (over z, x_hi, core).
Axes of the slice: x: 4 (x_hi: 2, x_lo: 2; x = x_hi * 2 + x_lo), y: 8, z: 8, core: 2. Of those that a mesh axis runs over, the one named last changes fastest.
Arguments:
- charges: bfloat16 [16384, 128], P(('blk', 'cluster')), may hold values from -6 to 6
- near_vals: bfloat16 [16384, 3, 128, 128], P(('blk', 'cluster')), may hold values from -0.3125 to 0.3125
- near_cols: int32 [16384, 3], P(('blk', 'cluster')), may hold values from 0 to 16383, as said below
- source_basis: bfloat16 [16384, 64, 128], P(('blk', 'cluster')), may hold values from -0.5 to 0.5
- target_basis: bfloat16 [16384, 64, 128], P(('blk', 'cluster')), may hold values from -0.75 to 0.75
- coupling: bfloat16 [16384, 2, 64, 64], P(('blk', 'cluster')), may hold values from -0.5 to 0.5
- far_cols: int32 [16384, 2], P(('blk', 'cluster')), may hold values from 0 to 16383, as said below
Outputs:
- potential_one: float32 [16384, 128], P(('blk', 'cluster'))
- potential_two: float32 [16384, 128], P(('blk', 'cluster'))
The draws below stay inside these ranges and needn't reach their ends.
Inputs may be any that keep to these rules, and one draw needn't show every extreme that they name: near_cols[i, 0] is block i itself; every entry names a block whose device has the same cluster index as block i's device and a blk index at most 3 away from it around the closed loop of blk. `far_cols`: every entry names a block whose device has the same blk index as block i's device; among the entries of one device's block rows at most 6 name blocks of any one cluster index, and exactly 6 name those of one cluster index.
All inputs are finite; a program needn't handle non-finite values.
Results may differ from the reference program's by a relative error of at most 0.004.
Values may be sent and summed in bfloat16 or wider, within the bound.
No kernel may reach another device: no remote copies, remote signals or barrier semaphores. Data moves between devices by JAX's collectives and lax.ppermute only.
A program may use at most 64 MiB of HBM per device.

```python
import jax
import jax.numpy as jnp
from jax import lax

PANELS = 128
RANK = 64
BLK_DEV = 32
KN = 3
KF = 2
REACH = 3
CAP = 6
NBLK = 16384
N_BLK = 16
N_CLUSTER = 32


def draw_near_cols(key, part):
    key_a, key_b = jax.random.split(jax.random.fold_in(key, 11))
    row_ids = jnp.arange(NBLK, dtype=jnp.int32)
    group_id = row_ids // BLK_DEV
    own_blk = group_id // N_CLUSTER
    own_cluster = group_id % N_CLUSTER
    offset = jax.random.randint(key_a, (NBLK, KN), -REACH, REACH + 1).astype(jnp.int32)
    within = jax.random.randint(key_b, (NBLK, KN), 0, BLK_DEV).astype(jnp.int32)
    column = jnp.arange(KN, dtype=jnp.int32)[None, :]
    offset = jnp.where(column == 0, 0, offset)
    within = jnp.where(column == 0, (row_ids % BLK_DEV)[:, None], within)
    target_blk = (own_blk[:, None] + offset + N_BLK) % N_BLK
    return ((target_blk * N_CLUSTER + own_cluster[:, None]) * BLK_DEV + within).astype(jnp.int32)


def draw_far_cols(key, part):
    entries = BLK_DEV * KF
    count_groups = N_BLK * N_CLUSTER

    def one_group(group_key, group_id):
        key_a, key_b, key_c, key_d = jax.random.split(group_key, 4)
        busiest = jax.random.randint(key_a, (), 0, N_CLUSTER).astype(jnp.int32)
        shuffled = jax.random.permutation(key_b, (N_CLUSTER - 1) * CAP).astype(jnp.int32)
        others = shuffled[:entries - CAP] // CAP
        others = others + (others >= busiest).astype(jnp.int32)
        owners = jnp.concatenate([jnp.full((CAP,), busiest, jnp.int32), others])
        owners = owners[jax.random.permutation(key_c, entries)]
        within = jax.random.randint(key_d, (entries,), 0, BLK_DEV).astype(jnp.int32)
        own_blk = group_id // N_CLUSTER
        return ((own_blk * N_CLUSTER + owners) * BLK_DEV + within).astype(jnp.int32)
    group_keys = jax.random.split(jax.random.fold_in(key, 23), count_groups)
    drawn = jax.vmap(one_group)(group_keys, jnp.arange(count_groups, dtype=jnp.int32))
    return drawn.reshape(NBLK, KF)


def levels(own_key, extent, pieces, smallest, high):
    gain, own = 1.0, jax.random.fold_in(own_key, 6)
    for position, blocks in pieces:
        draws = jnp.exp(jax.random.uniform(jax.random.fold_in(own, position), (blocks,), jnp.float32, smallest / len(pieces), high / len(pieces)))
        gain = gain * jnp.repeat(draws, extent[position] // blocks).reshape([-1 if axis == position else 1 for axis in range(len(extent))])
    return gain


def noise(stream_key, dims, deviation, bound, shards=(), held_as=jnp.bfloat16):
    values = jax.random.normal(stream_key, dims, jnp.float32) * deviation
    if len(shards) > 0:
        values = levels(stream_key, dims, shards, -0.22, 0.18) * values
    return jnp.clip(values, min=-bound, max=bound).astype(held_as)


def setup_inputs(seed: int = 0) -> dict:
    arg_keys = jax.random.split(jax.random.key(seed), 8)
    return {
        "charges": noise(arg_keys[0], (NBLK, PANELS), 1.0, 6.0, ((0, 512),)),
        "near_vals": noise(arg_keys[1], (NBLK, KN, PANELS, PANELS), (PANELS * KN) ** -0.5, 0.3125, ((0, 512),)),
        "near_cols": draw_near_cols(jax.random.fold_in(arg_keys[7], 71), 0),
        "source_basis": noise(arg_keys[3], (NBLK, RANK, PANELS), PANELS ** -0.5, 0.5, ((0, 512),)),
        "target_basis": noise(arg_keys[4], (NBLK, RANK, PANELS), RANK ** -0.5, 0.75, ((0, 512),)),
        "coupling": noise(arg_keys[5], (NBLK, KF, RANK, RANK), (RANK * KF) ** -0.5, 0.5, ((0, 512),)),
        "far_cols": draw_far_cols(jax.random.fold_in(arg_keys[7], 71), 0),
    }


def by_groups(function, arrays):
    shaped = tuple(a.reshape((a.shape[0] // BLK_DEV, BLK_DEV) + a.shape[1:]) for a in arrays)
    result = lax.map(lambda group_args: function(*group_args), shaped)
    return result.reshape((result.shape[0] * BLK_DEV,) + result.shape[2:])


def apply_operator(charge, near_vals, near_cols, source_basis, target_basis, coupling, far_cols):
    def moment_group(basis, field):
        return jnp.einsum("brp,bp->br", basis.astype(jnp.float32), field.astype(jnp.float32))

    moments = by_groups(moment_group, (source_basis, charge))

    def potential_group(blocks, cols, couple, fcols, tbasis):
        near_in = charge[cols].astype(jnp.float32)
        near_part = jnp.einsum("bkpq,bkq->bp", blocks.astype(jnp.float32), near_in)
        far_in = moments[fcols]
        coupled = jnp.einsum("bkrs,bks->br", couple.astype(jnp.float32), far_in,
                             precision=lax.Precision.HIGHEST).astype(jnp.bfloat16)
        far_part = jnp.einsum("brp,br->bp", tbasis.astype(jnp.float32), coupled.astype(jnp.float32))
        return near_part + far_part

    return by_groups(potential_group, (near_vals, near_cols, coupling, far_cols, target_basis))


def reference(charges, near_vals, near_cols, source_basis, target_basis, coupling, far_cols):
    potential_one = apply_operator(charges, near_vals, near_cols, source_basis, target_basis, coupling, far_cols)
    second = potential_one.astype(jnp.bfloat16)
    potential_two = apply_operator(second, near_vals, near_cols, source_basis, target_basis, coupling, far_cols)
    return potential_one, potential_two
```

```python
import jax
import jax.numpy as jnp
from jax import lax
from jax.sharding import PartitionSpec as P


def spread(block, axis):
    size = lax.axis_size(axis)
    copies = jnp.broadcast_to(block[None], (size,) + block.shape)
    return lax.all_to_all(copies, axis, 0, 0, tiled=True)


def shards(charges, near_vals, near_cols, source_basis, target_basis, coupling, far_cols):
    owners = lax.axis_size("cluster")
    cycle_size = lax.axis_size("blk")
    rows, panels = charges.shape
    rank = source_basis.shape[1]
    half = rows // 2
    near_group = near_cols // rows
    near_row = (near_group // owners) * rows + near_cols % rows
    near_hot = (near_row.reshape(-1)[:, None] == jnp.arange(cycle_size * rows)[None, :]).astype(jnp.bfloat16)
    far_owner = far_cols // rows % owners
    far_within = far_cols % rows
    far_row = far_owner * half + far_within % half
    far_upper = (far_within >= half)[:, :, None]
    far_hot = (far_row.reshape(-1)[:, None] == jnp.arange(owners * half)[None, :]).astype(jnp.bfloat16)

    def apply_operator(charge):
        window = spread(charge, "blk").reshape(cycle_size * rows, panels)
        moments = jnp.einsum("brp,bp->br", source_basis, charge, preferred_element_type=jnp.float32)
        packed = jnp.concatenate([moments[:half], moments[half:]], axis=1).astype(jnp.bfloat16)
        every_moment = spread(packed, "cluster").reshape(owners * half, 2 * rank)
        far_both = jnp.dot(far_hot, every_moment, preferred_element_type=jnp.float32).reshape(rows, -1, 2 * rank)
        far_in = jnp.where(far_upper, far_both[:, :, rank:], far_both[:, :, :rank]).astype(jnp.bfloat16)
        near_in = jnp.dot(near_hot, window, preferred_element_type=jnp.float32).astype(jnp.bfloat16)
        near_in = near_in.reshape(rows, -1, panels)
        near_part = jnp.einsum(
            "bkpq,bkq->bp", near_vals, near_in, preferred_element_type=jnp.float32
        )
        coupled = jnp.einsum(
            "bkrs,bks->br", coupling, far_in, preferred_element_type=jnp.float32
        ).astype(jnp.bfloat16)
        far_part = jnp.einsum(
            "brp,br->bp", target_basis, coupled, preferred_element_type=jnp.float32
        )
        return near_part + far_part

    potential_one = apply_operator(charges)
    potential_two = apply_operator(potential_one.astype(jnp.bfloat16))
    return (potential_one, potential_two)


def solution(mesh):
    in_specs = (
        P(("blk", "cluster"), None),
        P(("blk", "cluster"), None, None, None),
        P(("blk", "cluster"), None),
        P(("blk", "cluster"), None, None),
        P(("blk", "cluster"), None, None),
        P(("blk", "cluster"), None, None, None),
        P(("blk", "cluster"), None),
    )
    out_specs = (P(("blk", "cluster"), None), P(("blk", "cluster"), None))
    return jax.shard_map(shards, mesh=mesh, in_specs=in_specs, out_specs=out_specs, check_vma=False)
```

```python
import functools

import jax
import jax.numpy as jnp
from jax import lax
from jax.experimental import pallas as pl
from jax.experimental.pallas import tpu as pltpu
from jax.sharding import PartitionSpec as P

F32 = jnp.float32
BF16 = jnp.bfloat16
NT = (((1,), (1,)), ((), ()))
NN = (((1,), (0,)), ((), ()))
TILE = 256


def mul(a, b, dims):
    return lax.dot_general(a, b, dims, preferred_element_type=F32)


def iota(shape, dim):
    return lax.broadcasted_iota(jnp.int32, shape, dim)


def pick(index, depth):
    rows = index.shape[0]
    return jnp.where(iota((rows, depth), 1) == index, 1.0, 0.0).astype(BF16)


def packed_moments(field, source_ref, rank):
    rows, panels = field.shape
    total = jnp.zeros((rows, panels), F32)
    for base in range(0, source_ref.shape[0], TILE):
        product = mul(field, source_ref[base:base + TILE, :], NT)
        owner = (iota(product.shape, 1) + base) // rank
        product = jnp.where(owner == iota(product.shape, 0), product, 0.0)
        for lane in range(0, TILE, panels):
            total = total + product[:, lane:lane + panels]
    pair = jnp.where(iota((rows // 2, rows), 1) // 2 == iota((rows // 2, rows), 0), 1.0, 0.0)
    return mul(pair.astype(BF16), total.astype(BF16), NN).astype(BF16)


def first_kernel(rank, charge_ref, source_ref, copies_ref):
    packed = packed_moments(charge_ref[...], source_ref, rank)
    copies_ref[...] = jnp.broadcast_to(packed[None], copies_ref.shape)


def near_kernel(cycle_size, owners, pos_ref, cols_ref, low_ref, mid_ref, high_ref, vals_ref, near_ref):
    rows, panels = near_ref.shape
    kinds = cols_ref.shape[1]
    cols = cols_ref[...]
    target = lax.div(cols, jnp.int32(rows * owners))
    offset = lax.rem(target - pos_ref[0] + (cycle_size + 4), jnp.int32(cycle_size))
    row = offset * rows + lax.rem(cols, jnp.int32(rows))
    span = 3 * rows
    fields = []
    for k in range(kinds):
        index = row[:, k:k + 1]
        field = mul(pick(index, span), low_ref[...], NN)
        field = field + mul(pick(index - span, span), mid_ref[...], NN)
        field = field + mul(pick(index - 2 * span, span), high_ref[...], NN)
        fields.append(field.astype(BF16))
    group = 16
    for base in range(0, rows, group):
        parts = [field[base:base + group] for field in fields]
        total = jnp.zeros((group, panels), F32)
        for i in range(group):
            product = mul(parts[0], vals_ref[base + i, 0], NT)
            for k in range(1, kinds):
                product = product + mul(parts[k], vals_ref[base + i, k], NT)
            total = jnp.where(iota((group, panels), 0) == i, product, total)
        near_ref[base:base + group, :] = total


def potential(owners, rank, cols_ref, moments_ref, coupling_ref, target_ref, near_ref):
    rows, panels = near_ref.shape
    cols = cols_ref[...]
    owner = lax.rem(lax.div(cols, jnp.int32(rows)), jnp.int32(owners))
    within = lax.rem(cols, jnp.int32(rows))
    row = owner * (rows // 2) + lax.div(within, jnp.int32(2))
    upper = lax.rem(within, jnp.int32(2))
    lane_upper = iota((rows, panels), 1) // rank
    far_in = jnp.zeros((rows, panels), F32)
    for k in range(2):
        both = mul(pick(row[:, k:k + 1], moments_ref.shape[0]), moments_ref[...], NN)
        moved = jnp.where(upper[:, k:k + 1] == k, both, pltpu.roll(both, rank, 1))
        far_in = jnp.where(lane_upper == k, moved, far_in)
    far_in = far_in.astype(BF16)
    total = near_ref[...]
    for base in range(0, coupling_ref.shape[0], TILE):
        coupled = mul(far_in, coupling_ref[base:base + TILE, :], NT)
        block = (iota(coupled.shape, 1) + base) // rank
        coupled = jnp.where(block == iota(coupled.shape, 0), coupled, 0.0).astype(BF16)
        total = total + mul(coupled, target_ref[base:base + TILE, :], NN)
    return total


def middle_kernel(owners, rank, cols_ref, moments_ref, coupling_ref, target_ref, near_ref, source_ref,
                  potential_ref, second_ref, copies_ref):
    total = potential(owners, rank, cols_ref, moments_ref, coupling_ref, target_ref, near_ref)
    potential_ref[...] = total
    second = total.astype(BF16)
    second_ref[...] = second
    packed = packed_moments(second, source_ref, rank)
    copies_ref[...] = jnp.broadcast_to(packed[None], copies_ref.shape)


def last_kernel(owners, rank, cols_ref, moments_ref, coupling_ref, target_ref, near_ref, potential_ref):
    potential_ref[...] = potential(owners, rank, cols_ref, moments_ref, coupling_ref, target_ref, near_ref)


def call(kernel, outs, scalars=0):
    vmem = pl.BlockSpec(memory_space=pltpu.VMEM)

    def run(*operands):
        specs = [pl.BlockSpec(memory_space=pltpu.SMEM)] * scalars + [vmem] * (len(operands) - scalars)
        return pl.pallas_call(
            kernel,
            out_shape=outs,
            in_specs=specs,
            out_specs=jax.tree.map(lambda _: vmem, outs),
            compiler_params=pltpu.CompilerParams(vmem_limit_bytes=16 << 20),
        )(*operands)

    return run


def from_behind(block, axis, distance):
    size = lax.axis_size(axis)
    return lax.ppermute(block, axis, [((i - distance) % size, i) for i in range(size)])


def shards(charges, near_vals, near_cols, source_basis, target_basis, coupling, far_cols):
    owners = lax.axis_size("cluster")
    cycle_size = lax.axis_size("blk")
    rows, panels = charges.shape
    rank = source_basis.shape[1]
    pos = lax.axis_index("blk").reshape(1)
    source = source_basis.reshape(rows * rank, panels)
    target = target_basis.reshape(rows * rank, panels)
    coupling = coupling.transpose(0, 2, 1, 3).reshape(rows * rank, 2 * rank)
    copies = jax.ShapeDtypeStruct((owners, rows // 2, 2 * rank), BF16)
    field32 = jax.ShapeDtypeStruct((rows, panels), F32)
    field16 = jax.ShapeDtypeStruct((rows, panels), BF16)

    def far_exchange(copies):
        return lax.all_to_all(copies, "cluster", 0, 0, tiled=True).reshape(-1, 2 * rank)

    def near_part(charge):
        mid = jnp.concatenate([from_behind(charge, "blk", 1), charge, from_behind(charge, "blk", -1)], axis=0)
        low = from_behind(mid, "blk", 3)
        high = from_behind(mid, "blk", -3)
        run = call(functools.partial(near_kernel, cycle_size, owners), field32, 1)
        return run(pos, near_cols, low, mid, high, near_vals)

    first = call(functools.partial(first_kernel, rank), copies)(charges, source)
    near = near_part(charges)
    moments = far_exchange(first)
    middle = call(functools.partial(middle_kernel, owners, rank), (field32, field16, copies))
    potential_one, second, sent = middle(far_cols, moments, coupling, target, near, source)
    near = near_part(second)
    moments = far_exchange(sent)
    potential_two = call(functools.partial(last_kernel, owners, rank), field32)(far_cols, moments, coupling, target, near)
    return (potential_one, potential_two)


def solution(mesh):
    in_specs = (
        P(("blk", "cluster"), None),
        P(("blk", "cluster"), None, None, None),
        P(("blk", "cluster"), None),
        P(("blk", "cluster"), None, None),
        P(("blk", "cluster"), None, None),
        P(("blk", "cluster"), None, None, None),
        P(("blk", "cluster"), None),
    )
    out_specs = (P(("blk", "cluster"), None), P(("blk", "cluster"), None))
    return jax.shard_map(shards, mesh=mesh, in_specs=in_specs, out_specs=out_specs, check_vma=False)
```

```python
import functools

import jax
import jax.numpy as jnp
from jax import lax
from jax.experimental import pallas as pl
from jax.experimental.pallas import tpu as pltpu
from jax.sharding import PartitionSpec as P

F32 = jnp.float32
BF16 = jnp.bfloat16
NT = (((1,), (1,)), ((), ()))
NN = (((1,), (0,)), ((), ()))
CHUNK = 4
LANES = 128


def mul(a, b, dims):
    return lax.dot_general(a, b, dims, preferred_element_type=F32)


def iota(shape, dim):
    return lax.broadcasted_iota(jnp.int32, shape, dim)


def pick(index, depth):
    rows = index.shape[0]
    return jnp.where(iota((rows, depth), 1) == index, 1.0, 0.0).astype(BF16)


def column(row):
    size = row.shape[1]
    square = (size, size)
    spread = jnp.broadcast_to(row.astype(F32), square)
    chosen = jnp.where(iota(square, 0) == iota(square, 1), spread, 0.0)
    return jnp.sum(chosen, axis=1, keepdims=True).astype(jnp.int32)


def padded(field):
    rows = field.shape[0]
    return jnp.concatenate([field, jnp.zeros((LANES - rows, field.shape[1]), field.dtype)], axis=0)


def own_columns(blocks, height, product):
    total = jnp.zeros((height, LANES), F32)
    lane = iota((height, LANES), 1)
    for base in range(0, blocks, CHUNK):
        result = product(base)
        for i in range(CHUNK):
            total = jnp.where(lane == base + i, result[i * height:(i + 1) * height], total)
    return total


def send_moments(field, source_ref, copies_ref):
    blocks = field.shape[0]
    rank = source_ref.shape[0] // blocks
    wide = padded(field)

    def product(base):
        return mul(source_ref[base * rank:(base + CHUNK) * rank, :], wide, NT)

    moments = own_columns(blocks, rank, product)
    moments = jnp.concatenate([moments, jnp.zeros((LANES - rank, LANES), F32)], axis=0).T
    half = blocks // 2
    packed = moments[:half] + pltpu.roll(moments[half:blocks], rank, 1)
    copies_ref[...] = jnp.broadcast_to(packed.astype(BF16)[None], copies_ref.shape)


def first_kernel(charge_hbm, source_hbm, target_hbm, coupling_hbm, copies_ref, source_ref, target_ref, coupling_ref,
                 charge_ref, sems):
    pairs = [(charge_hbm, charge_ref), (source_hbm, source_ref), (coupling_hbm, coupling_ref), (target_hbm, target_ref)]
    moves = [pltpu.make_async_copy(a, b, sems.at[n]) for n, (a, b) in enumerate(pairs)]
    for move in moves:
        move.start()
    moves[0].wait()
    moves[1].wait()
    send_moments(charge_ref[...], source_ref, copies_ref)
    moves[2].wait()
    moves[3].wait()


def moments_kernel(field_ref, source_ref, copies_ref):
    send_moments(field_ref[...], source_ref, copies_ref)


def fetch(source, dest, sems):
    moves = []
    for n in range(dest.shape[0] // CHUNK):
        part = pl.ds(n * CHUNK, CHUNK)
        moves.append(pltpu.make_async_copy(source.at[part], dest.at[part], sems.at[n]))
    for move in moves:
        move.start()
    return moves


def own_kernel(field_ref, vals_hbm, near_ref, vals_ref, sems):
    blocks, panels = field_ref.shape
    moves = fetch(vals_hbm.at[:, pl.ds(0, 1)], vals_ref, sems)
    wide = padded(field_ref[...])

    def product(base):
        moves[base // CHUNK].wait()
        return mul(vals_ref[base:base + CHUNK, 0].reshape(CHUNK * panels, panels), wide, NT)

    near_ref[...] = own_columns(blocks, panels, product).T[:blocks]


def near_kernel(cycle_size, owners, pos_ref, cols_ref, low_ref, high_ref, vals_hbm, own_ref, near_ref, vals_ref, sems):
    blocks, panels = own_ref.shape
    moves = fetch(vals_hbm.at[:, pl.ds(1, vals_ref.shape[1])], vals_ref, sems)
    kinds = cols_ref.shape[0]
    cols = cols_ref[...]
    target = lax.div(cols, jnp.int32(blocks * owners))
    offset = lax.rem(target - pos_ref[0] + (cycle_size + 3), jnp.int32(cycle_size))
    row = offset * blocks + lax.rem(cols, jnp.int32(blocks))
    span = low_ref.shape[0]
    fields = []
    for k in range(1, kinds):
        index = column(row[k:k + 1])
        field = mul(pick(index, span), low_ref[...], NN)
        beyond = jnp.where(index >= span, index - (span - blocks), -1)
        field = field + mul(pick(beyond, span), high_ref[...], NN)
        fields.append(field.astype(BF16))
    wide = padded(jnp.concatenate(fields, axis=1))

    def product(base):
        moves[base // CHUNK].wait()
        vals = [vals_ref[base:base + CHUNK, k].reshape(CHUNK * panels, panels) for k in range(kinds - 1)]
        return mul(jnp.concatenate(vals, axis=1), wide, NT)

    near_ref[...] = own_ref[...] + own_columns(blocks, panels, product).T[:blocks]


def potential(owners, cols_ref, moments_ref, coupling_ref, target_ref, near_ref):
    blocks, panels = near_ref.shape
    kinds = cols_ref.shape[0]
    rank = coupling_ref.shape[2]
    half = blocks // 2
    cols = cols_ref[...]
    owner = lax.rem(lax.div(cols, jnp.int32(blocks)), jnp.int32(owners))
    within = lax.rem(cols, jnp.int32(blocks))
    row = owner * half + lax.rem(within, jnp.int32(half))
    upper = lax.div(within, jnp.int32(half))
    fields = []
    for k in range(kinds):
        both = mul(pick(column(row[k:k + 1]), moments_ref.shape[0]), moments_ref[...], NN)
        both = jnp.where(column(upper[k:k + 1]) == 1, pltpu.roll(both, rank, 1), both)
        fields.append(padded(both[:, :rank].astype(BF16)))

    def product(base):
        result = None
        for k in range(kinds):
            couple = coupling_ref[base:base + CHUNK, k].reshape(CHUNK * rank, rank)
            part = mul(couple, fields[k], NT)
            result = part if result is None else result + part
        return result

    coupled = own_columns(blocks, rank, product)
    coupled = jnp.concatenate([coupled, coupled], axis=0).T[:blocks]
    total = near_ref[...]
    step = 2 * LANES
    wide = jnp.concatenate([coupled, coupled], axis=1)
    for base in range(0, target_ref.shape[0], step):
        block = (iota(wide.shape, 1) + base) // rank
        kept = jnp.where(block == iota(wide.shape, 0), wide, 0.0).astype(BF16)
        total = total + mul(kept, target_ref[base:base + step, :], NN)
    return total


def middle_kernel(owners, cols_ref, moments_ref, coupling_ref, target_ref, near_ref, potential_ref, second_ref):
    total = potential(owners, cols_ref, moments_ref, coupling_ref, target_ref, near_ref)
    potential_ref[...] = total
    second_ref[...] = total.astype(BF16)


def last_kernel(owners, cols_ref, moments_ref, coupling_ref, target_ref, near_ref, potential_ref):
    potential_ref[...] = potential(owners, cols_ref, moments_ref, coupling_ref, target_ref, near_ref)


VMEM = pl.BlockSpec(memory_space=pltpu.VMEM)
SMEM = pl.BlockSpec(memory_space=pltpu.SMEM)
HBM = pl.BlockSpec(memory_space=pltpu.HBM)


def call(kernel, outs, *operands, specs=None, scratch=(), flops=0, moved=0):
    return pl.pallas_call(
        kernel,
        out_shape=outs,
        in_specs=specs or [VMEM] * len(operands),
        out_specs=[VMEM] * len(outs) if isinstance(outs, tuple) else VMEM,
        scratch_shapes=scratch,
        compiler_params=pltpu.CompilerParams(vmem_limit_bytes=16 << 20),
        cost_estimate=pl.CostEstimate(flops=flops, bytes_accessed=moved, transcendentals=0),
    )(*operands)


def from_behind(block, axis, distance):
    size = lax.axis_size(axis)
    return lax.ppermute(block, axis, [((i - distance) % size, i) for i in range(size)])


def shards(charges, near_vals, near_cols, source_basis, target_basis, coupling, far_cols):
    owners = lax.axis_size("cluster")
    cycle_size = lax.axis_size("blk")
    blocks, panels = charges.shape
    rank = source_basis.shape[1]
    pos = lax.axis_index("blk").reshape(1)
    near_cols = near_cols.T
    far_cols = far_cols.T
    shape = jax.ShapeDtypeStruct
    basis = shape((blocks * rank, panels), BF16)
    copies = shape((owners, blocks // 2, 2 * rank), BF16)
    field32 = shape((blocks, panels), F32)
    field16 = shape((blocks, panels), BF16)
    tile = 2 * blocks * panels * panels

    def far_exchange(copies):
        return lax.all_to_all(copies, "cluster", 0, 0, tiled=True).reshape(-1, 2 * rank)

    def near_part(charge, behind):
        own = call(own_kernel, field32, charge, near_vals, specs=[VMEM, HBM], scratch=stage(1), flops=32 * tile, moved=tile)
        pair = jnp.concatenate([behind, charge], axis=0)
        low = jnp.concatenate([from_behind(pair, "blk", 2), pair], axis=0)
        high = from_behind(low, "blk", -3)
        kernel = functools.partial(near_kernel, cycle_size, owners)
        return call(kernel, field32, pos, near_cols, low, high, near_vals, own,
                    specs=[SMEM] + [VMEM] * 3 + [HBM, VMEM], scratch=stage(near_vals.shape[1] - 1), flops=64 * tile, moved=2 * tile)

    def stage(kinds):
        return [pltpu.VMEM((blocks, kinds, panels, panels), BF16), pltpu.SemaphoreType.DMA((blocks // CHUNK,))]

    def pinned(place, *arrays):
        return [pltpu.with_memory_space_constraint(array, place) for array in arrays]

    near_vals, = pinned(pltpu.HBM, near_vals)
    kept = pltpu.VMEM(basis.shape, BF16)
    operands = (charges, source_basis.reshape(basis.shape), target_basis.reshape(basis.shape), coupling)
    sent, source, target, coupling = call(
        first_kernel, (copies, kept, kept, pltpu.VMEM(coupling.shape, BF16)), *pinned(pltpu.HBM, *operands),
        specs=[HBM] * 4, scratch=[pltpu.VMEM(charges.shape, BF16), pltpu.SemaphoreType.DMA((4,))],
        flops=16 * tile, moved=2 * tile)
    source, target, coupling = pinned(pltpu.VMEM, source, target, coupling)
    behind, sent = lax.optimization_barrier((from_behind(charges, "blk", 1), sent))
    near = near_part(charges, behind)
    moments = far_exchange(sent)
    potential_one, second = call(functools.partial(middle_kernel, owners), (field32, field16),
                                 far_cols, moments, coupling, target, near, flops=48 * tile, moved=tile)
    sent = call(moments_kernel, copies, second, source, flops=16 * tile, moved=tile)
    behind, sent = lax.optimization_barrier((from_behind(second, "blk", 1), sent))
    near = near_part(second, behind)
    moments = far_exchange(sent)
    potential_two = call(functools.partial(last_kernel, owners), field32,
                         far_cols, moments, coupling, target, near, flops=48 * tile, moved=tile)
    return (potential_one, potential_two)


def solution(mesh):
    in_specs = (
        P(("blk", "cluster"), None),
        P(("blk", "cluster"), None, None, None),
        P(("blk", "cluster"), None),
        P(("blk", "cluster"), None, None),
        P(("blk", "cluster"), None, None),
        P(("blk", "cluster"), None, None, None),
        P(("blk", "cluster"), None),
    )
    out_specs = (P(("blk", "cluster"), None), P(("blk", "cluster"), None))
    return jax.shard_map(shards, mesh=mesh, in_specs=in_specs, out_specs=out_specs, check_vma=False)
```

```python
import functools

import jax
import jax.numpy as jnp
from jax import lax
from jax.experimental import pallas as pl
from jax.experimental.pallas import tpu as pltpu
from jax.sharding import PartitionSpec as P

F32 = jnp.float32
BF16 = jnp.bfloat16
NT = (((1,), (1,)), ((), ()))
NN = (((1,), (0,)), ((), ()))
CHUNK = 4
LANES = 128


def mul(a, b, dims):
    return lax.dot_general(a, b, dims, preferred_element_type=F32)


def iota(shape, dim):
    return lax.broadcasted_iota(jnp.int32, shape, dim)


def pick(index, depth):
    rows = index.shape[0]
    return jnp.where(iota((rows, depth), 1) == index, 1.0, 0.0).astype(BF16)


def column(row):
    size = row.shape[1]
    square = (size, size)
    spread = jnp.broadcast_to(row.astype(F32), square)
    chosen = jnp.where(iota(square, 0) == iota(square, 1), spread, 0.0)
    return jnp.sum(chosen, axis=1, keepdims=True).astype(jnp.int32)


def padded(field):
    rows = field.shape[0]
    return jnp.concatenate([field, jnp.zeros((LANES - rows, field.shape[1]), field.dtype)], axis=0)


def own_columns(blocks, height, product):
    total = jnp.zeros((height, LANES), F32)
    lane = iota((height, LANES), 1)
    for base in range(0, blocks, CHUNK):
        result = product(base)
        for i in range(CHUNK):
            total = jnp.where(lane == base + i, result[i * height:(i + 1) * height], total)
    return total


def send_moments(field, source_ref, copies_ref):
    blocks = field.shape[0]
    rank = source_ref.shape[0] // blocks
    wide = padded(field)

    def product(base):
        return mul(source_ref[base * rank:(base + CHUNK) * rank, :], wide, NT)

    moments = own_columns(blocks, rank, product)
    moments = jnp.concatenate([moments, jnp.zeros((LANES - rank, LANES), F32)], axis=0).T
    half = blocks // 2
    packed = moments[:half] + pltpu.roll(moments[half:blocks], rank, 1)
    copies_ref[...] = jnp.broadcast_to(packed.astype(BF16)[None], copies_ref.shape)


def spread_kernel(field_ref, copies_ref):
    copies_ref[...] = jnp.broadcast_to(field_ref[...][None], copies_ref.shape)


def first_kernel(charge_hbm, source_hbm, target_hbm, coupling_hbm, copies_ref, source_ref, target_ref, coupling_ref,
                 charge_ref, sems):
    pairs = [(charge_hbm, charge_ref), (source_hbm, source_ref), (coupling_hbm, coupling_ref), (target_hbm, target_ref)]
    moves = [pltpu.make_async_copy(a, b, sems.at[n]) for n, (a, b) in enumerate(pairs)]
    for move in moves:
        move.start()
    moves[0].wait()
    moves[1].wait()
    send_moments(charge_ref[...], source_ref, copies_ref)
    moves[2].wait()
    moves[3].wait()


def moments_kernel(field_ref, source_ref, copies_ref):
    send_moments(field_ref[...], source_ref, copies_ref)


def fetch(source, dest, sems):
    moves = []
    for n in range(dest.shape[0] // CHUNK):
        part = pl.ds(n * CHUNK, CHUNK)
        moves.append(pltpu.make_async_copy(source.at[part], dest.at[part], sems.at[n]))
    for move in moves:
        move.start()
    return moves


def own_kernel(field_ref, vals_hbm, near_ref, vals_ref, sems):
    blocks, panels = field_ref.shape
    moves = fetch(vals_hbm.at[:, pl.ds(0, 1)], vals_ref, sems)
    wide = padded(field_ref[...])

    def product(base):
        moves[base // CHUNK].wait()
        return mul(vals_ref[base:base + CHUNK, 0].reshape(CHUNK * panels, panels), wide, NT)

    near_ref[...] = own_columns(blocks, panels, product).T[:blocks]


def near_kernel(owners, cols_ref, window_ref, vals_hbm, own_ref, near_ref, vals_ref, sems):
    blocks, panels = own_ref.shape
    moves = fetch(vals_hbm.at[:, pl.ds(1, vals_ref.shape[1])], vals_ref, sems)
    kinds = cols_ref.shape[0]
    cols = cols_ref[...]
    row = lax.div(cols, jnp.int32(blocks * owners)) * blocks + lax.rem(cols, jnp.int32(blocks))
    fields = []
    for k in range(1, kinds):
        chosen = pick(column(row[k:k + 1]), window_ref.shape[0])
        fields.append(mul(chosen, window_ref[...], NN).astype(BF16))
    wide = padded(jnp.concatenate(fields, axis=1))

    def product(base):
        moves[base // CHUNK].wait()
        vals = [vals_ref[base:base + CHUNK, k].reshape(CHUNK * panels, panels) for k in range(kinds - 1)]
        return mul(jnp.concatenate(vals, axis=1), wide, NT)

    near_ref[...] = own_ref[...] + own_columns(blocks, panels, product).T[:blocks]


def potential(owners, cols_ref, moments_ref, coupling_ref, target_ref, near_ref):
    blocks, panels = near_ref.shape
    kinds = cols_ref.shape[0]
    rank = coupling_ref.shape[2]
    half = blocks // 2
    cols = cols_ref[...]
    owner = lax.rem(lax.div(cols, jnp.int32(blocks)), jnp.int32(owners))
    within = lax.rem(cols, jnp.int32(blocks))
    row = owner * half + lax.rem(within, jnp.int32(half))
    upper = lax.div(within, jnp.int32(half))
    fields = []
    for k in range(kinds):
        both = mul(pick(column(row[k:k + 1]), moments_ref.shape[0]), moments_ref[...], NN)
        both = jnp.where(column(upper[k:k + 1]) == 1, pltpu.roll(both, rank, 1), both)
        fields.append(padded(both[:, :rank].astype(BF16)))

    def product(base):
        result = None
        for k in range(kinds):
            couple = coupling_ref[base:base + CHUNK, k].reshape(CHUNK * rank, rank)
            part = mul(couple, fields[k], NT)
            result = part if result is None else result + part
        return result

    coupled = own_columns(blocks, rank, product)
    coupled = jnp.concatenate([coupled, coupled], axis=0).T[:blocks]
    total = near_ref[...]
    step = 2 * LANES
    wide = jnp.concatenate([coupled, coupled], axis=1)
    for base in range(0, target_ref.shape[0], step):
        block = (iota(wide.shape, 1) + base) // rank
        kept = jnp.where(block == iota(wide.shape, 0), wide, 0.0).astype(BF16)
        total = total + mul(kept, target_ref[base:base + step, :], NN)
    return total


def middle_kernel(owners, cols_ref, moments_ref, coupling_ref, target_ref, near_ref,
                  potential_ref, second_ref, copies_ref):
    total = potential(owners, cols_ref, moments_ref, coupling_ref, target_ref, near_ref)
    potential_ref[...] = total
    second = total.astype(BF16)
    second_ref[...] = second
    copies_ref[...] = jnp.broadcast_to(second[None], copies_ref.shape)


def last_kernel(owners, cols_ref, moments_ref, coupling_ref, target_ref, near_ref, potential_ref):
    potential_ref[...] = potential(owners, cols_ref, moments_ref, coupling_ref, target_ref, near_ref)


VMEM = pl.BlockSpec(memory_space=pltpu.VMEM)
SMEM = pl.BlockSpec(memory_space=pltpu.SMEM)
HBM = pl.BlockSpec(memory_space=pltpu.HBM)


def call(kernel, outs, *operands, specs=None, scratch=(), flops=0, moved=0):
    return pl.pallas_call(
        kernel,
        out_shape=outs,
        in_specs=specs or [VMEM] * len(operands),
        out_specs=[VMEM] * len(outs) if isinstance(outs, tuple) else VMEM,
        scratch_shapes=scratch,
        compiler_params=pltpu.CompilerParams(vmem_limit_bytes=16 << 20),
        cost_estimate=pl.CostEstimate(flops=flops, bytes_accessed=moved, transcendentals=0),
    )(*operands)


def shards(charges, near_vals, near_cols, source_basis, target_basis, coupling, far_cols):
    owners = lax.axis_size("cluster")
    cycle_size = lax.axis_size("blk")
    blocks, panels = charges.shape
    rank = source_basis.shape[1]
    near_cols = near_cols.T
    far_cols = far_cols.T
    shape = jax.ShapeDtypeStruct
    basis = shape((blocks * rank, panels), BF16)
    copies = shape((owners, blocks // 2, 2 * rank), BF16)
    spread = shape((cycle_size, blocks, panels), BF16)
    field32 = shape((blocks, panels), F32)
    field16 = shape((blocks, panels), BF16)
    tile = 2 * blocks * panels * panels

    def far_exchange(copies):
        return lax.all_to_all(copies, "cluster", 0, 0, tiled=True).reshape(-1, 2 * rank)

    def near_exchange(copies):
        return lax.all_to_all(copies, "blk", 0, 0, tiled=True).reshape(-1, panels)

    def own_part(charge):
        return call(own_kernel, field32, charge, near_vals, specs=[VMEM, HBM], scratch=stage(1), flops=32 * tile, moved=tile)

    def near_part(window, own):
        return call(functools.partial(near_kernel, owners), field32, near_cols, window, near_vals, own,
                    specs=[VMEM] * 2 + [HBM, VMEM], scratch=stage(near_vals.shape[1] - 1), flops=64 * tile, moved=2 * tile)

    def stage(kinds):
        return [pltpu.VMEM((blocks, kinds, panels, panels), BF16), pltpu.SemaphoreType.DMA((blocks // CHUNK,))]

    def pinned(place, *arrays):
        return [pltpu.with_memory_space_constraint(array, place) for array in arrays]

    near_vals, = pinned(pltpu.HBM, near_vals)
    kept = pltpu.VMEM(basis.shape, BF16)
    operands = (charges, source_basis.reshape(basis.shape), target_basis.reshape(basis.shape), coupling)
    sent, source, target, coupling = call(
        first_kernel, (copies, kept, kept, pltpu.VMEM(coupling.shape, BF16)), *pinned(pltpu.HBM, *operands),
        specs=[HBM] * 4, scratch=[pltpu.VMEM(charges.shape, BF16), pltpu.SemaphoreType.DMA((4,))],
        flops=16 * tile, moved=2 * tile)
    source, target, coupling = pinned(pltpu.VMEM, source, target, coupling)
    window = near_exchange(call(spread_kernel, spread, charges, moved=tile))
    own = own_part(charges)
    window, sent, own = lax.optimization_barrier((window, sent, own))
    moments = far_exchange(sent)
    near = near_part(window, own)
    potential_one, second, spread_second = call(
        functools.partial(middle_kernel, owners), (field32, field16, spread),
        far_cols, moments, coupling, target, near, flops=48 * tile, moved=tile)
    window = near_exchange(spread_second)
    sent = call(moments_kernel, copies, second, source, flops=16 * tile, moved=tile)
    own = own_part(second)
    window, sent, own = lax.optimization_barrier((window, sent, own))
    moments = far_exchange(sent)
    near = near_part(window, own)
    potential_two = call(functools.partial(last_kernel, owners), field32,
                         far_cols, moments, coupling, target, near, flops=48 * tile, moved=tile)
    return (potential_one, potential_two)


def solution(mesh):
    in_specs = (
        P(("blk", "cluster"), None),
        P(("blk", "cluster"), None, None, None),
        P(("blk", "cluster"), None),
        P(("blk", "cluster"), None, None),
        P(("blk", "cluster"), None, None),
        P(("blk", "cluster"), None, None, None),
        P(("blk", "cluster"), None),
    )
    out_specs = (P(("blk", "cluster"), None), P(("blk", "cluster"), None))
    return jax.shard_map(shards, mesh=mesh, in_specs=in_specs, out_specs=out_specs, check_vma=False)
```

```python
import functools

import jax
import jax.numpy as jnp
from jax import lax
from jax.experimental import pallas as pl
from jax.experimental.pallas import tpu as pltpu
from jax.sharding import PartitionSpec as P

F32 = jnp.float32
BF16 = jnp.bfloat16
NT = (((1,), (1,)), ((), ()))
NN = (((1,), (0,)), ((), ()))
CHUNK = 4
LANES = 128


def mul(a, b, dims):
    return lax.dot_general(a, b, dims, preferred_element_type=F32)


def iota(shape, dim):
    return lax.broadcasted_iota(jnp.int32, shape, dim)


def pick(index, depth):
    rows = index.shape[0]
    return jnp.where(iota((rows, depth), 1) == index, 1.0, 0.0).astype(BF16)


def column(row):
    size = row.shape[1]
    square = (size, size)
    spread = jnp.broadcast_to(row.astype(F32), square)
    chosen = jnp.where(iota(square, 0) == iota(square, 1), spread, 0.0)
    return jnp.sum(chosen, axis=1, keepdims=True).astype(jnp.int32)


def padded(field):
    rows = field.shape[0]
    return jnp.concatenate([field, jnp.zeros((LANES - rows, field.shape[1]), field.dtype)], axis=0)


def own_columns(blocks, height, product):
    total = jnp.zeros((height, LANES), F32)
    lane = iota((height, LANES), 1)
    for base in range(0, blocks, CHUNK):
        result = product(base)
        for i in range(CHUNK):
            total = jnp.where(lane == base + i, result[i * height:(i + 1) * height], total)
    return total


def send_moments(field, source_ref, copies_ref):
    blocks = field.shape[0]
    rank = source_ref.shape[0] // blocks
    wide = padded(field)

    def product(base):
        return mul(source_ref[base * rank:(base + CHUNK) * rank, :], wide, NT)

    moments = own_columns(blocks, rank, product)
    moments = jnp.concatenate([moments, jnp.zeros((LANES - rank, LANES), F32)], axis=0).T
    half = blocks // 2
    packed = moments[:half] + pltpu.roll(moments[half:blocks], rank, 1)
    copies_ref[...] = jnp.broadcast_to(packed.astype(BF16)[None], copies_ref.shape)


def first_kernel(charge_hbm, source_hbm, target_hbm, coupling_hbm,
                 copies_ref, charge_ref, source_ref, target_ref, coupling_ref, sems):
    pairs = [(charge_hbm, charge_ref), (source_hbm, source_ref), (coupling_hbm, coupling_ref), (target_hbm, target_ref)]
    moves = [pltpu.make_async_copy(a, b, sems.at[n]) for n, (a, b) in enumerate(pairs)]
    for move in moves:
        move.start()
    moves[0].wait()
    moves[1].wait()
    send_moments(charge_ref[...], source_ref, copies_ref)
    moves[2].wait()
    moves[3].wait()


def fetch(source, dest, sems):
    moves = []
    for n in range(dest.shape[0] // CHUNK):
        part = pl.ds(n * CHUNK, CHUNK)
        moves.append(pltpu.make_async_copy(source.at[part], dest.at[part], sems.at[n]))
    for move in moves:
        move.start()
    return moves


def near_product(fields, vals_ref):
    blocks, panels = fields[0].shape
    wide = padded(jnp.concatenate(fields, axis=1))

    def product(base):
        vals = [vals_ref[base:base + CHUNK, k].reshape(CHUNK * panels, panels) for k in range(len(fields))]
        return mul(jnp.concatenate(vals, axis=1), wide, NT)

    return own_columns(blocks, panels, product).T[:blocks]


def own_kernel(field_ref, vals_hbm, near_ref, vals_ref, sems):
    for move in fetch(vals_hbm.at[:, pl.ds(0, 1)], vals_ref, sems):
        move.wait()
    near_ref[...] = near_product([field_ref[...]], vals_ref)


def near_first_kernel(cycle_size, owners, pos_ref, cols_ref, low_ref, high_ref, vals_hbm, own_ref, near_ref, vals_ref, sems):
    blocks = own_ref.shape[0]
    kinds = cols_ref.shape[0]
    moves = fetch(vals_hbm.at[:, pl.ds(1, kinds - 1)], vals_ref, sems)
    cols = cols_ref[...]
    target = lax.div(cols, jnp.int32(blocks * owners))
    offset = lax.rem(target - pos_ref[0] + (cycle_size + 3), jnp.int32(cycle_size))
    row = offset * blocks + lax.rem(cols, jnp.int32(blocks))
    span = low_ref.shape[0]
    fields = []
    for k in range(1, kinds):
        index = column(row[k:k + 1])
        field = mul(pick(index, span), low_ref[...], NN)
        beyond = jnp.where(index >= span, index - (span - blocks), -1)
        field = field + mul(pick(beyond, span), high_ref[...], NN)
        fields.append(field.astype(BF16))
    for move in moves:
        move.wait()
    near_ref[...] = own_ref[...] + near_product(fields, vals_ref)


def near_kernel(owners, cols_ref, field_ref, window_ref, vals_hbm, near_ref, vals_ref, sems):
    moves = fetch(vals_hbm, vals_ref, sems)
    blocks = field_ref.shape[0]
    cols = cols_ref[...]
    row = lax.div(cols, jnp.int32(blocks * owners)) * blocks + lax.rem(cols, jnp.int32(blocks))
    fields = [field_ref[...]]
    for k in range(1, cols_ref.shape[0]):
        chosen = pick(column(row[k:k + 1]), window_ref.shape[0])
        fields.append(mul(chosen, window_ref[...], NN).astype(BF16))
    for move in moves:
        move.wait()
    near_ref[...] = near_product(fields, vals_ref)


def potential(owners, cols_ref, moments_ref, coupling_ref, target_ref, near_ref):
    blocks, panels = near_ref.shape
    kinds = cols_ref.shape[0]
    rank = coupling_ref.shape[2]
    half = blocks // 2
    cols = cols_ref[...]
    owner = lax.rem(lax.div(cols, jnp.int32(blocks)), jnp.int32(owners))
    within = lax.rem(cols, jnp.int32(blocks))
    row = owner * half + lax.rem(within, jnp.int32(half))
    upper = lax.div(within, jnp.int32(half))
    fields = []
    for k in range(kinds):
        both = mul(pick(column(row[k:k + 1]), moments_ref.shape[0]), moments_ref[...], NN)
        both = jnp.where(column(upper[k:k + 1]) == 1, pltpu.roll(both, rank, 1), both)
        fields.append(padded(both[:, :rank].astype(BF16)))

    def product(base):
        result = None
        for k in range(kinds):
            couple = coupling_ref[base:base + CHUNK, k].reshape(CHUNK * rank, rank)
            part = mul(couple, fields[k], NT)
            result = part if result is None else result + part
        return result

    coupled = own_columns(blocks, rank, product)
    coupled = jnp.concatenate([coupled, coupled], axis=0).T[:blocks]
    total = near_ref[...]
    step = 2 * LANES
    wide = jnp.concatenate([coupled, coupled], axis=1)
    for base in range(0, target_ref.shape[0], step):
        block = (iota(wide.shape, 1) + base) // rank
        kept = jnp.where(block == iota(wide.shape, 0), wide, 0.0).astype(BF16)
        total = total + mul(kept, target_ref[base:base + step, :], NN)
    return total


def middle_kernel(owners, cols_ref, moments_ref, coupling_ref, target_ref, near_ref, source_ref,
                  potential_ref, second_ref, spread_ref, copies_ref):
    total = potential(owners, cols_ref, moments_ref, coupling_ref, target_ref, near_ref)
    potential_ref[...] = total
    second = total.astype(BF16)
    second_ref[...] = second
    spread_ref[...] = jnp.broadcast_to(second[None], spread_ref.shape)
    send_moments(second, source_ref, copies_ref)


def last_kernel(owners, cols_ref, moments_ref, coupling_ref, target_ref, near_ref, potential_ref):
    potential_ref[...] = potential(owners, cols_ref, moments_ref, coupling_ref, target_ref, near_ref)


VMEM = pl.BlockSpec(memory_space=pltpu.VMEM)
SMEM = pl.BlockSpec(memory_space=pltpu.SMEM)
HBM = pl.BlockSpec(memory_space=pltpu.HBM)


def call(kernel, outs, *operands, specs=None, scratch=(), flops=0, moved=0):
    return pl.pallas_call(
        kernel,
        out_shape=outs,
        in_specs=specs or [VMEM] * len(operands),
        out_specs=[VMEM] * len(outs) if isinstance(outs, tuple) else VMEM,
        scratch_shapes=scratch,
        compiler_params=pltpu.CompilerParams(vmem_limit_bytes=16 << 20),
        cost_estimate=pl.CostEstimate(flops=flops, bytes_accessed=moved, transcendentals=0),
    )(*operands)


def from_behind(block, axis, distance):
    size = lax.axis_size(axis)
    return lax.ppermute(block, axis, [((i - distance) % size, i) for i in range(size)])


def shards(charges, near_vals, near_cols, source_basis, target_basis, coupling, far_cols):
    owners = lax.axis_size("cluster")
    cycle_size = lax.axis_size("blk")
    blocks, panels = charges.shape
    rank = source_basis.shape[1]
    pos = lax.axis_index("blk").reshape(1)
    near_cols = near_cols.T
    far_cols = far_cols.T
    shape = jax.ShapeDtypeStruct
    basis = shape((blocks * rank, panels), BF16)
    copies = shape((owners, blocks // 2, 2 * rank), BF16)
    spread = shape((cycle_size, blocks, panels), BF16)
    field32 = shape((blocks, panels), F32)
    field16 = shape((blocks, panels), BF16)
    tile = 2 * blocks * panels * panels

    def stage(kinds):
        return [pltpu.VMEM((blocks, kinds, panels, panels), BF16), pltpu.SemaphoreType.DMA((blocks // CHUNK,))]

    def pinned(place, *arrays):
        return [pltpu.with_memory_space_constraint(array, place) for array in arrays]

    def far_exchange(copies):
        return lax.all_to_all(copies, "cluster", 0, 0, tiled=True).reshape(-1, 2 * rank)

    kept = pltpu.VMEM(basis.shape, BF16)
    kinds = near_vals.shape[1]
    near_vals, = pinned(pltpu.HBM, near_vals)
    operands = (charges, source_basis.reshape(basis.shape), target_basis.reshape(basis.shape), coupling)
    sent, charge, source, target, coupling = call(
        first_kernel, (copies, pltpu.VMEM(charges.shape, BF16), kept, kept, pltpu.VMEM(coupling.shape, BF16)),
        *pinned(pltpu.HBM, *operands), specs=[HBM] * 4, scratch=[pltpu.SemaphoreType.DMA((4,))],
        flops=16 * tile, moved=2 * tile)
    source, target, coupling = pinned(pltpu.VMEM, source, target, coupling)

    behind, sent = lax.optimization_barrier((from_behind(charges, "blk", 1), sent))
    own = call(own_kernel, field32, charge, near_vals, specs=[VMEM, HBM], scratch=stage(1), flops=32 * tile, moved=tile)
    pair = jnp.concatenate([behind, charge], axis=0)
    low = jnp.concatenate([from_behind(pair, "blk", 2), pair], axis=0)
    high = from_behind(low, "blk", -3)
    near = call(functools.partial(near_first_kernel, cycle_size, owners), field32,
                pos, near_cols, low, high, near_vals, own, specs=[SMEM] + [VMEM] * 3 + [HBM, VMEM],
                scratch=stage(kinds - 1), flops=64 * tile, moved=2 * tile)
    moments = far_exchange(sent)
    potential_one, second, spread_second, sent = call(
        functools.partial(middle_kernel, owners), (field32, field16, spread, copies),
        far_cols, moments, coupling, target, near, source, flops=64 * tile, moved=tile)

    window = lax.all_to_all(spread_second, "blk", 0, 0, tiled=True).reshape(-1, panels)
    window, sent, second = lax.optimization_barrier((window, sent, second))
    moments = far_exchange(sent)
    near = call(functools.partial(near_kernel, owners), field32, near_cols, second, window, near_vals,
                specs=[VMEM] * 3 + [HBM], scratch=stage(kinds), flops=96 * tile, moved=3 * tile)
    potential_two = call(functools.partial(last_kernel, owners), field32,
                         far_cols, moments, coupling, target, near, flops=48 * tile, moved=tile)
    return (potential_one, potential_two)


def solution(mesh):
    in_specs = (
        P(("blk", "cluster"), None),
        P(("blk", "cluster"), None, None, None),
        P(("blk", "cluster"), None),
        P(("blk", "cluster"), None, None),
        P(("blk", "cluster"), None, None),
        P(("blk", "cluster"), None, None, None),
        P(("blk", "cluster"), None),
    )
    out_specs = (P(("blk", "cluster"), None), P(("blk", "cluster"), None))
    return jax.shard_map(shards, mesh=mesh, in_specs=in_specs, out_specs=out_specs, check_vma=False)
```

```python
import functools

import jax
import jax.numpy as jnp
from jax import lax
from jax.experimental import pallas as pl
from jax.experimental.pallas import tpu as pltpu
from jax.sharding import PartitionSpec as P

F32 = jnp.float32
BF16 = jnp.bfloat16
NT = (((1,), (1,)), ((), ()))
NN = (((1,), (0,)), ((), ()))
CHUNK = 4
LANES = 128


def mul(a, b, dims):
    return lax.dot_general(a, b, dims, preferred_element_type=F32)


def iota(shape, dim):
    return lax.broadcasted_iota(jnp.int32, shape, dim)


def pick(index, depth):
    rows = index.shape[0]
    return jnp.where(iota((rows, depth), 1) == index, 1.0, 0.0).astype(BF16)


def column(row):
    size = row.shape[1]
    square = (size, size)
    spread = jnp.broadcast_to(row.astype(F32), square)
    chosen = jnp.where(iota(square, 0) == iota(square, 1), spread, 0.0)
    return jnp.sum(chosen, axis=1, keepdims=True).astype(jnp.int32)


def padded(field):
    rows = field.shape[0]
    return jnp.concatenate([field, jnp.zeros((LANES - rows, field.shape[1]), field.dtype)], axis=0)


def own_columns(blocks, height, product):
    total = jnp.zeros((height, LANES), F32)
    lane = iota((height, LANES), 1)
    for base in range(0, blocks, CHUNK):
        result = product(base)
        for i in range(CHUNK):
            total = jnp.where(lane == base + i, result[i * height:(i + 1) * height], total)
    return total


def send_moments(field, source_ref, copies_ref):
    blocks = field.shape[0]
    rank = source_ref.shape[0] // blocks
    wide = padded(field)

    def product(base):
        return mul(source_ref[base * rank:(base + CHUNK) * rank, :], wide, NT)

    moments = own_columns(blocks, rank, product)
    moments = jnp.concatenate([moments, jnp.zeros((LANES - rank, LANES), F32)], axis=0).T
    half = blocks // 2
    packed = moments[:half] + pltpu.roll(moments[half:blocks], rank, 1)
    copies_ref[...] = jnp.broadcast_to(packed.astype(BF16)[None], copies_ref.shape)


def moments_kernel(field_ref, source_ref, copies_ref):
    send_moments(field_ref[...], source_ref, copies_ref)


def first_kernel(charge_hbm, source_hbm, target_hbm, coupling_hbm,
                 copies_ref, charge_ref, source_ref, target_ref, coupling_ref, sems):
    pairs = [(charge_hbm, charge_ref), (source_hbm, source_ref), (coupling_hbm, coupling_ref), (target_hbm, target_ref)]
    moves = [pltpu.make_async_copy(a, b, sems.at[n]) for n, (a, b) in enumerate(pairs)]
    for move in moves:
        move.start()
    moves[0].wait()
    moves[1].wait()
    send_moments(charge_ref[...], source_ref, copies_ref)
    moves[2].wait()
    moves[3].wait()


def fetch(source, dest, sems):
    moves = []
    for n in range(dest.shape[0] // CHUNK):
        part = pl.ds(n * CHUNK, CHUNK)
        moves.append(pltpu.make_async_copy(source.at[part], dest.at[part], sems.at[n]))
    for move in moves:
        move.start()
    return moves


def near_product(fields, vals_ref):
    blocks, panels = fields[0].shape
    wide = padded(jnp.concatenate(fields, axis=1))

    def product(base):
        vals = [vals_ref[base:base + CHUNK, k].reshape(CHUNK * panels, panels) for k in range(len(fields))]
        return mul(jnp.concatenate(vals, axis=1), wide, NT)

    return own_columns(blocks, panels, product).T[:blocks]


def own_kernel(field_ref, vals_hbm, near_ref, vals_ref, sems):
    for move in fetch(vals_hbm.at[:, pl.ds(0, 1)], vals_ref, sems):
        move.wait()
    near_ref[...] = near_product([field_ref[...]], vals_ref)


def own_store_kernel(field_ref, vals_hbm, kept_ref, near_ref, stored_ref, vals_ref, sems):
    moves = fetch(vals_hbm.at[:, pl.ds(0, 1)], vals_ref, sems)
    stored_ref[...] = kept_ref[...]
    for move in moves:
        move.wait()
    near_ref[...] = near_product([field_ref[...]], vals_ref)


def near_kernel(cycle_size, owners, pos_ref, cols_ref, low_ref, high_ref, vals_hbm, own_ref, near_ref, vals_ref, sems):
    blocks = own_ref.shape[0]
    kinds = cols_ref.shape[0]
    moves = fetch(vals_hbm.at[:, pl.ds(1, kinds - 1)], vals_ref, sems)
    cols = cols_ref[...]
    target = lax.div(cols, jnp.int32(blocks * owners))
    offset = lax.rem(target - pos_ref[0] + (cycle_size + 3), jnp.int32(cycle_size))
    row = offset * blocks + lax.rem(cols, jnp.int32(blocks))
    span = low_ref.shape[0]
    fields = []
    for k in range(1, kinds):
        index = column(row[k:k + 1])
        field = mul(pick(index, span), low_ref[...], NN)
        beyond = jnp.where(index >= span, index - (span - blocks), -1)
        field = field + mul(pick(beyond, span), high_ref[...], NN)
        fields.append(field.astype(BF16))
    for move in moves:
        move.wait()
    near_ref[...] = own_ref[...] + near_product(fields, vals_ref)


def potential(owners, cols_ref, moments_ref, coupling_ref, target_ref, near_ref):
    blocks, panels = near_ref.shape
    kinds = cols_ref.shape[0]
    rank = coupling_ref.shape[2]
    half = blocks // 2
    cols = cols_ref[...]
    owner = lax.rem(lax.div(cols, jnp.int32(blocks)), jnp.int32(owners))
    within = lax.rem(cols, jnp.int32(blocks))
    row = owner * half + lax.rem(within, jnp.int32(half))
    upper = lax.div(within, jnp.int32(half))
    fields = []
    for k in range(kinds):
        both = mul(pick(column(row[k:k + 1]), moments_ref.shape[0]), moments_ref[...], NN)
        both = jnp.where(column(upper[k:k + 1]) == 1, pltpu.roll(both, rank, 1), both)
        fields.append(padded(both[:, :rank].astype(BF16)))

    def product(base):
        result = None
        for k in range(kinds):
            couple = coupling_ref[base:base + CHUNK, k].reshape(CHUNK * rank, rank)
            part = mul(couple, fields[k], NT)
            result = part if result is None else result + part
        return result

    coupled = own_columns(blocks, rank, product)
    coupled = jnp.concatenate([coupled, coupled], axis=0).T[:blocks]
    total = near_ref[...]
    step = 2 * LANES
    wide = jnp.concatenate([coupled, coupled], axis=1)
    for base in range(0, target_ref.shape[0], step):
        block = (iota(wide.shape, 1) + base) // rank
        kept = jnp.where(block == iota(wide.shape, 0), wide, 0.0).astype(BF16)
        total = total + mul(kept, target_ref[base:base + step, :], NN)
    return total


def middle_kernel(owners, cols_ref, moments_ref, coupling_ref, target_ref, near_ref, potential_ref, second_ref):
    total = potential(owners, cols_ref, moments_ref, coupling_ref, target_ref, near_ref)
    potential_ref[...] = total
    second_ref[...] = total.astype(BF16)


def last_kernel(owners, cols_ref, moments_ref, coupling_ref, target_ref, near_ref, potential_ref):
    potential_ref[...] = potential(owners, cols_ref, moments_ref, coupling_ref, target_ref, near_ref)


VMEM = pl.BlockSpec(memory_space=pltpu.VMEM)
SMEM = pl.BlockSpec(memory_space=pltpu.SMEM)
HBM = pl.BlockSpec(memory_space=pltpu.HBM)


def call(kernel, outs, *operands, specs=None, scratch=(), flops=0, moved=0):
    return pl.pallas_call(
        kernel,
        out_shape=outs,
        in_specs=specs or [VMEM] * len(operands),
        out_specs=[VMEM] * len(outs) if isinstance(outs, tuple) else VMEM,
        scratch_shapes=scratch,
        compiler_params=pltpu.CompilerParams(vmem_limit_bytes=16 << 20),
        cost_estimate=pl.CostEstimate(flops=flops, bytes_accessed=moved, transcendentals=0),
    )(*operands)


def from_behind(block, axis, distance):
    size = lax.axis_size(axis)
    return lax.ppermute(block, axis, [((i - distance) % size, i) for i in range(size)])


def shards(charges, near_vals, near_cols, source_basis, target_basis, coupling, far_cols):
    owners = lax.axis_size("cluster")
    cycle_size = lax.axis_size("blk")
    blocks, panels = charges.shape
    rank = source_basis.shape[1]
    pos = lax.axis_index("blk").reshape(1)
    near_cols = near_cols.T
    far_cols = far_cols.T
    shape = jax.ShapeDtypeStruct
    basis = shape((blocks * rank, panels), BF16)
    copies = shape((owners, blocks // 2, 2 * rank), BF16)
    field32 = shape((blocks, panels), F32)
    field16 = shape((blocks, panels), BF16)
    tile = 2 * blocks * panels * panels

    def stage(kinds):
        return [pltpu.VMEM((blocks, kinds, panels, panels), BF16), pltpu.SemaphoreType.DMA((blocks // CHUNK,))]

    def pinned(place, *arrays):
        return [pltpu.with_memory_space_constraint(array, place) for array in arrays]

    def far_exchange(copies):
        return lax.all_to_all(copies, "cluster", 0, 0, tiled=True).reshape(-1, 2 * rank)

    kept = pltpu.VMEM(basis.shape, BF16)
    kinds = near_vals.shape[1]
    near_vals, = pinned(pltpu.HBM, near_vals)
    operands = (charges, source_basis.reshape(basis.shape), target_basis.reshape(basis.shape), coupling)
    sent, charge, source, target, coupling = call(
        first_kernel, (copies, pltpu.VMEM(charges.shape, BF16), kept, kept, pltpu.VMEM(coupling.shape, BF16)),
        *pinned(pltpu.HBM, *operands), specs=[HBM] * 4, scratch=[pltpu.SemaphoreType.DMA((4,))],
        flops=16 * tile, moved=2 * tile)
    source, target, coupling = pinned(pltpu.VMEM, source, target, coupling)

    def exchange(sent, field, behind, own):
        behind, sent = lax.optimization_barrier((behind, sent))
        pair = jnp.concatenate([behind, field], axis=0)
        low = jnp.concatenate([from_behind(pair, "blk", 2), pair], axis=0)
        high = from_behind(low, "blk", -3)
        near = call(functools.partial(near_kernel, cycle_size, owners), field32,
                    pos, near_cols, low, high, near_vals, own, specs=[SMEM] + [VMEM] * 3 + [HBM, VMEM],
                    scratch=stage(kinds - 1), flops=64 * tile, moved=2 * tile)
        return far_exchange(sent), near

    own = call(own_kernel, field32, charge, near_vals, specs=[VMEM, HBM], scratch=stage(1), flops=32 * tile, moved=tile)
    moments, near = exchange(sent, charge, from_behind(charges, "blk", 1), own)
    total, second = call(functools.partial(middle_kernel, owners), (pltpu.VMEM(charges.shape, F32), field16),
                                 far_cols, moments, coupling, target, near, flops=48 * tile, moved=tile)
    sent = call(moments_kernel, copies, second, source, flops=16 * tile, moved=tile)
    own, potential_one = call(own_store_kernel, (field32, field32), second, near_vals, *pinned(pltpu.VMEM, total),
                              specs=[VMEM, HBM, VMEM], scratch=stage(1), flops=32 * tile, moved=tile)
    moments, near = exchange(sent, second, from_behind(second, "blk", 1), own)
    potential_two = call(functools.partial(last_kernel, owners), field32,
                         far_cols, moments, coupling, target, near, flops=48 * tile, moved=tile)
    return (potential_one, potential_two)


def solution(mesh):
    in_specs = (
        P(("blk", "cluster"), None),
        P(("blk", "cluster"), None, None, None),
        P(("blk", "cluster"), None),
        P(("blk", "cluster"), None, None),
        P(("blk", "cluster"), None, None),
        P(("blk", "cluster"), None, None, None),
        P(("blk", "cluster"), None),
    )
    out_specs = (P(("blk", "cluster"), None), P(("blk", "cluster"), None))
    return jax.shard_map(shards, mesh=mesh, in_specs=in_specs, out_specs=out_specs, check_vma=False)
```

```python
import functools

import jax
import jax.numpy as jnp
from jax import lax
from jax.experimental import pallas as pl
from jax.experimental.pallas import tpu as pltpu
from jax.sharding import PartitionSpec as P

F32 = jnp.float32
BF16 = jnp.bfloat16
NT = (((1,), (1,)), ((), ()))
NN = (((1,), (0,)), ((), ()))
CHUNK = 4
LANES = 128


def mul(a, b, dims):
    return lax.dot_general(a, b, dims, preferred_element_type=F32)


def iota(shape, dim):
    return lax.broadcasted_iota(jnp.int32, shape, dim)


def pick(index, depth):
    rows = index.shape[0]
    return jnp.where(iota((rows, depth), 1) == index, 1.0, 0.0).astype(BF16)


def column(row):
    size = row.shape[1]
    square = (size, size)
    spread = jnp.broadcast_to(row.astype(F32), square)
    chosen = jnp.where(iota(square, 0) == iota(square, 1), spread, 0.0)
    return jnp.sum(chosen, axis=1, keepdims=True).astype(jnp.int32)


def padded(field):
    rows = field.shape[0]
    return jnp.concatenate([field, jnp.zeros((LANES - rows, field.shape[1]), field.dtype)], axis=0)


def own_columns(blocks, height, product):
    total = jnp.zeros((height, LANES), F32)
    lane = iota((height, LANES), 1)
    for base in range(0, blocks, CHUNK):
        result = product(base)
        for i in range(CHUNK):
            total = jnp.where(lane == base + i, result[i * height:(i + 1) * height], total)
    return total


def send_moments(field, source_ref, copies_ref):
    blocks = field.shape[0]
    rank = source_ref.shape[0] // blocks
    wide = padded(field)

    def product(base):
        return mul(source_ref[base * rank:(base + CHUNK) * rank, :], wide, NT)

    moments = own_columns(blocks, rank, product)
    moments = jnp.concatenate([moments, jnp.zeros((LANES - rank, LANES), F32)], axis=0).T
    half = blocks // 2
    packed = moments[:half] + pltpu.roll(moments[half:blocks], rank, 1)
    copies_ref[...] = jnp.broadcast_to(packed.astype(BF16)[None], copies_ref.shape)


def moments_kernel(field_ref, source_hbm, copies_ref, source_ref, sem):
    move = pltpu.make_async_copy(source_hbm, source_ref, sem)
    move.start()
    move.wait()
    send_moments(field_ref[...], source_ref, copies_ref)


def first_kernel(charge_hbm, source_hbm, target_hbm, coupling_hbm,
                 copies_ref, charge_ref, target_ref, packed_ref, source_ref, coupling_ref, sems):
    pairs = [(charge_hbm, charge_ref), (source_hbm, source_ref), (coupling_hbm, coupling_ref), (target_hbm, target_ref)]
    moves = [pltpu.make_async_copy(a, b, sems.at[n]) for n, (a, b) in enumerate(pairs)]
    for move in moves:
        move.start()
    moves[0].wait()
    moves[1].wait()
    send_moments(charge_ref[...], source_ref, copies_ref)
    moves[2].wait()
    blocks, kinds, rank, _ = coupling_ref.shape
    for i in range(blocks):
        packed_ref[i * rank:(i + 1) * rank, :] = jnp.concatenate([coupling_ref[i, k] for k in range(kinds)], axis=1)
    moves[3].wait()


def fetch(source, dest, sems):
    moves = []
    for n in range(dest.shape[0] // CHUNK):
        part = pl.ds(n * CHUNK, CHUNK)
        moves.append(pltpu.make_async_copy(source.at[part], dest.at[part], sems.at[n]))
    for move in moves:
        move.start()
    return moves


def near_product(fields, vals_ref):
    blocks, panels = fields[0].shape
    wide = padded(jnp.concatenate(fields, axis=1))

    def product(base):
        vals = [vals_ref[base:base + CHUNK, k].reshape(CHUNK * panels, panels) for k in range(len(fields))]
        return mul(jnp.concatenate(vals, axis=1), wide, NT)

    return own_columns(blocks, panels, product).T[:blocks]


def own_kernel(field_ref, vals_hbm, near_ref, rest_ref, vals_ref, sems, rest_sems):
    moves = fetch(vals_hbm.at[:, pl.ds(0, 1)], vals_ref, sems)
    rest = fetch(vals_hbm.at[:, pl.ds(1, rest_ref.shape[1])], rest_ref, rest_sems)
    for move in moves:
        move.wait()
    near_ref[...] = near_product([field_ref[...]], vals_ref)
    for move in rest:
        move.wait()


def own_store_kernel(field_ref, vals_hbm, kept_ref, near_ref, rest_ref, stored_ref, vals_ref, sems, rest_sems):
    stored_ref[...] = kept_ref[...]
    own_kernel(field_ref, vals_hbm, near_ref, rest_ref, vals_ref, sems, rest_sems)


def near_kernel(cycle_size, owners, pos_ref, cols_ref, low_ref, high_ref, vals_ref, own_ref, near_ref):
    blocks = own_ref.shape[0]
    kinds = cols_ref.shape[0]
    cols = cols_ref[...]
    target = lax.div(cols, jnp.int32(blocks * owners))
    offset = lax.rem(target - pos_ref[0] + (cycle_size + 3), jnp.int32(cycle_size))
    row = offset * blocks + lax.rem(cols, jnp.int32(blocks))
    span = low_ref.shape[0]
    fields = []
    for k in range(1, kinds):
        index = column(row[k:k + 1])
        field = mul(pick(index, span), low_ref[...], NN)
        beyond = jnp.where(index >= span, index - (span - blocks), -1)
        field = field + mul(pick(beyond, span), high_ref[...], NN)
        fields.append(field.astype(BF16))
    near_ref[...] = own_ref[...] + near_product(fields, vals_ref)


def potential(owners, cols_ref, moments_ref, coupling_ref, target_ref, near_ref):
    blocks, panels = near_ref.shape
    kinds = cols_ref.shape[0]
    rank = coupling_ref.shape[0] // blocks
    half = blocks // 2
    cols = cols_ref[...]
    owner = lax.rem(lax.div(cols, jnp.int32(blocks)), jnp.int32(owners))
    within = lax.rem(cols, jnp.int32(blocks))
    row = owner * half + lax.rem(within, jnp.int32(half))
    upper = lax.div(within, jnp.int32(half))
    fields = []
    for k in range(kinds):
        both = mul(pick(column(row[k:k + 1]), moments_ref.shape[0]), moments_ref[...], NN)
        both = jnp.where(column(upper[k:k + 1]) == 1, pltpu.roll(both, rank, 1), both)
        fields.append(both[:, :rank].astype(BF16))
    wide = padded(jnp.concatenate(fields, axis=1))

    def product(base):
        return mul(coupling_ref[base * rank:(base + CHUNK) * rank, :], wide, NT)

    coupled = own_columns(blocks, rank, product)
    coupled = jnp.concatenate([coupled, coupled], axis=0).T[:blocks]
    total = near_ref[...]
    step = 2 * LANES
    wide = jnp.concatenate([coupled, coupled], axis=1)
    for base in range(0, target_ref.shape[0], step):
        block = (iota(wide.shape, 1) + base) // rank
        kept = jnp.where(block == iota(wide.shape, 0), wide, 0.0).astype(BF16)
        total = total + mul(kept, target_ref[base:base + step, :], NN)
    return total


def middle_kernel(owners, cols_ref, moments_ref, coupling_ref, target_ref, near_ref, potential_ref, second_ref):
    total = potential(owners, cols_ref, moments_ref, coupling_ref, target_ref, near_ref)
    potential_ref[...] = total
    second_ref[...] = total.astype(BF16)


def last_kernel(owners, cols_ref, moments_ref, coupling_ref, target_ref, near_ref, potential_ref):
    potential_ref[...] = potential(owners, cols_ref, moments_ref, coupling_ref, target_ref, near_ref)


VMEM = pl.BlockSpec(memory_space=pltpu.VMEM)
SMEM = pl.BlockSpec(memory_space=pltpu.SMEM)
HBM = pl.BlockSpec(memory_space=pltpu.HBM)


def call(kernel, outs, *operands, specs=None, scratch=(), flops=0, moved=0):
    return pl.pallas_call(
        kernel,
        out_shape=outs,
        in_specs=specs or [VMEM] * len(operands),
        out_specs=[VMEM] * len(outs) if isinstance(outs, tuple) else VMEM,
        scratch_shapes=scratch,
        compiler_params=pltpu.CompilerParams(vmem_limit_bytes=16 << 20),
        cost_estimate=pl.CostEstimate(flops=flops, bytes_accessed=moved, transcendentals=0),
    )(*operands)


def from_behind(block, axis, distance):
    size = lax.axis_size(axis)
    return lax.ppermute(block, axis, [((i - distance) % size, i) for i in range(size)])


def shards(charges, near_vals, near_cols, source_basis, target_basis, coupling, far_cols):
    owners = lax.axis_size("cluster")
    cycle_size = lax.axis_size("blk")
    blocks, panels = charges.shape
    rank = source_basis.shape[1]
    pos = lax.axis_index("blk").reshape(1)
    near_cols = near_cols.T
    far_cols = far_cols.T
    shape = jax.ShapeDtypeStruct
    basis = shape((blocks * rank, panels), BF16)
    copies = shape((owners, blocks // 2, 2 * rank), BF16)
    field32 = shape((blocks, panels), F32)
    field16 = shape((blocks, panels), BF16)
    tile = 2 * blocks * panels * panels

    def stage(kinds):
        return [pltpu.VMEM((blocks, kinds, panels, panels), BF16), pltpu.SemaphoreType.DMA((blocks // CHUNK,))]

    def pinned(place, *arrays):
        return [pltpu.with_memory_space_constraint(array, place) for array in arrays]

    def far_exchange(copies):
        return lax.all_to_all(copies, "cluster", 0, 0, tiled=True).reshape(-1, 2 * rank)

    kept = pltpu.VMEM(basis.shape, BF16)
    kinds = near_vals.shape[1]
    rest = pltpu.VMEM((blocks, kinds - 1, panels, panels), BF16)
    near_vals, charges_hbm, source, target, coupling = pinned(
        pltpu.HBM, near_vals, charges, source_basis.reshape(basis.shape), target_basis.reshape(basis.shape), coupling)
    sent, charge, target, coupling = call(
        first_kernel, (copies, pltpu.VMEM(charges.shape, BF16), kept, kept), charges_hbm, source, target, coupling,
        specs=[HBM] * 4, scratch=[kept, pltpu.VMEM(coupling.shape, BF16), pltpu.SemaphoreType.DMA((4,))],
        flops=16 * tile, moved=2 * tile)
    target, coupling = pinned(pltpu.VMEM, target, coupling)
    own_scratch = stage(1) + stage(1)[1:]

    def exchange(sent, field, behind, own, vals):
        behind, sent = lax.optimization_barrier((behind, sent))
        pair = jnp.concatenate([behind, field], axis=0)
        low = jnp.concatenate([from_behind(pair, "blk", 2), pair], axis=0)
        high = from_behind(low, "blk", -3)
        near = call(functools.partial(near_kernel, cycle_size, owners), field32,
                    pos, near_cols, low, high, *pinned(pltpu.VMEM, vals), own, specs=[SMEM] + [VMEM] * 5,
                    flops=64 * tile, moved=2 * tile)
        return far_exchange(sent), near

    own, vals = call(own_kernel, (field32, rest), charge, near_vals, specs=[VMEM, HBM], scratch=own_scratch,
                     flops=32 * tile, moved=3 * tile)
    moments, near = exchange(sent, charge, from_behind(charges, "blk", 1), own, vals)
    total, second = call(functools.partial(middle_kernel, owners), (pltpu.VMEM(charges.shape, F32), field16),
                         far_cols, moments, coupling, target, near, flops=48 * tile, moved=tile)
    sent = call(moments_kernel, copies, second, source, specs=[VMEM, HBM],
                scratch=[kept, pltpu.SemaphoreType.DMA(())], flops=16 * tile, moved=tile)
    own, vals, potential_one = call(
        own_store_kernel, (field32, rest, field32), second, near_vals, *pinned(pltpu.VMEM, total),
        specs=[VMEM, HBM, VMEM], scratch=own_scratch, flops=32 * tile, moved=3 * tile)
    moments, near = exchange(sent, second, from_behind(second, "blk", 1), own, vals)
    potential_two = call(functools.partial(last_kernel, owners), field32,
                         far_cols, moments, coupling, target, near, flops=48 * tile, moved=tile)
    return (potential_one, potential_two)


def solution(mesh):
    in_specs = (
        P(("blk", "cluster"), None),
        P(("blk", "cluster"), None, None, None),
        P(("blk", "cluster"), None),
        P(("blk", "cluster"), None, None),
        P(("blk", "cluster"), None, None),
        P(("blk", "cluster"), None, None, None),
        P(("blk", "cluster"), None),
    )
    out_specs = (P(("blk", "cluster"), None), P(("blk", "cluster"), None))
    return jax.shard_map(shards, mesh=mesh, in_specs=in_specs, out_specs=out_specs, check_vma=False)
```

```python
import functools

import jax
import jax.numpy as jnp
from jax import lax
from jax.experimental import pallas as pl
from jax.experimental.pallas import tpu as pltpu
from jax.sharding import PartitionSpec as P

F32 = jnp.float32
BF16 = jnp.bfloat16
NT = (((1,), (1,)), ((), ()))
NN = (((1,), (0,)), ((), ()))
CHUNK = 4
LANES = 128
CHAIN = (-3, 2, 1)


def mul(a, b, dims):
    return lax.dot_general(a, b, dims, preferred_element_type=F32)


def iota(shape, dim):
    return lax.broadcasted_iota(jnp.int32, shape, dim)


def pick(index, depth):
    rows = index.shape[0]
    return jnp.where(iota((rows, depth), 1) == index, 1.0, 0.0).astype(BF16)


def column(row):
    size = row.shape[1]
    square = (size, size)
    spread = jnp.broadcast_to(row.astype(F32), square)
    chosen = jnp.where(iota(square, 0) == iota(square, 1), spread, 0.0)
    return jnp.sum(chosen, axis=1, keepdims=True).astype(jnp.int32)


def padded(field):
    rows = field.shape[0]
    return jnp.concatenate([field, jnp.zeros((LANES - rows, field.shape[1]), field.dtype)], axis=0)


def own_columns(blocks, height, product):
    total = jnp.zeros((height, LANES), F32)
    lane = iota((height, LANES), 1)
    for base in range(0, blocks, CHUNK):
        result = product(base)
        for i in range(CHUNK):
            total = jnp.where(lane == base + i, result[i * height:(i + 1) * height], total)
    return total


def send_moments(field, source_ref, copies_ref):
    blocks = field.shape[0]
    rank = source_ref.shape[0] // blocks
    wide = padded(field)

    def product(base):
        return mul(source_ref[base * rank:(base + CHUNK) * rank, :], wide, NT)

    moments = own_columns(blocks, rank, product)
    moments = jnp.concatenate([moments, jnp.zeros((LANES - rank, LANES), F32)], axis=0).T
    half = blocks // 2
    packed = moments[:half] + pltpu.roll(moments[half:blocks], rank, 1)
    copies_ref[...] = jnp.broadcast_to(packed.astype(BF16)[None], copies_ref.shape)


def moments_kernel(field_ref, source_hbm, copies_ref, source_ref, sem):
    move = pltpu.make_async_copy(source_hbm, source_ref, sem)
    move.start()
    move.wait()
    send_moments(field_ref[...], source_ref, copies_ref)


def first_kernel(charge_hbm, source_hbm, target_hbm, coupling_hbm,
                 copies_ref, charge_ref, target_ref, packed_ref, source_ref, coupling_ref, sems):
    pairs = [(charge_hbm, charge_ref), (source_hbm, source_ref), (coupling_hbm, coupling_ref), (target_hbm, target_ref)]
    moves = [pltpu.make_async_copy(a, b, sems.at[n]) for n, (a, b) in enumerate(pairs)]
    for move in moves:
        move.start()
    moves[0].wait()
    moves[1].wait()
    send_moments(charge_ref[...], source_ref, copies_ref)
    moves[2].wait()
    blocks, kinds, rank, _ = coupling_ref.shape
    for i in range(blocks):
        packed_ref[i * rank:(i + 1) * rank, :] = jnp.concatenate([coupling_ref[i, k] for k in range(kinds)], axis=1)
    moves[3].wait()


def fetch(source, dest, sems):
    moves = []
    for n in range(dest.shape[0] // CHUNK):
        part = pl.ds(n * CHUNK, CHUNK)
        moves.append(pltpu.make_async_copy(source.at[part], dest.at[part], sems.at[n]))
    for move in moves:
        move.start()
    return moves


def near_product(fields, vals_ref):
    blocks, panels = fields[0].shape
    wide = padded(jnp.concatenate(fields, axis=1))

    def product(base):
        vals = [vals_ref[base:base + CHUNK, k].reshape(CHUNK * panels, panels) for k in range(len(fields))]
        return mul(jnp.concatenate(vals, axis=1), wide, NT)

    return own_columns(blocks, panels, product).T[:blocks]


def own_kernel(field_ref, vals_hbm, near_ref, rest_ref, vals_ref, sems, rest_sems):
    moves = fetch(vals_hbm.at[:, pl.ds(0, 1)], vals_ref, sems)
    rest = fetch(vals_hbm.at[:, pl.ds(1, rest_ref.shape[1])], rest_ref, rest_sems)
    for move in moves:
        move.wait()
    near_ref[...] = near_product([field_ref[...]], vals_ref)
    for move in rest:
        move.wait()


def own_store_kernel(field_ref, vals_hbm, kept_ref, near_ref, rest_ref, stored_ref, vals_ref, sems, rest_sems):
    stored_ref[...] = kept_ref[...]
    own_kernel(field_ref, vals_hbm, near_ref, rest_ref, vals_ref, sems, rest_sems)


def near_kernel(cycle_size, owners, order, pos_ref, cols_ref, low_ref, high_ref, vals_ref, own_ref, near_ref):
    blocks = own_ref.shape[0]
    kinds = cols_ref.shape[0]
    cols = cols_ref[...]
    target = lax.div(cols, jnp.int32(blocks * owners))
    offset = lax.rem(target - pos_ref[0] + cycle_size, jnp.int32(cycle_size))
    slot = jnp.zeros(cols.shape, jnp.int32)
    for place in range(len(order) - 1, -1, -1):
        slot = jnp.where(offset == order[place] % cycle_size, place, slot)
    row = slot * blocks + lax.rem(cols, jnp.int32(blocks))
    span = low_ref.shape[0]
    fields = []
    for k in range(1, kinds):
        index = column(row[k:k + 1])
        field = mul(pick(index, span), low_ref[...], NN)
        field = field + mul(pick(index - span, span), high_ref[...], NN)
        fields.append(field.astype(BF16))
    near_ref[...] = own_ref[...] + near_product(fields, vals_ref)


def potential(owners, cols_ref, moments_ref, coupling_ref, target_ref, near_ref):
    blocks, panels = near_ref.shape
    kinds = cols_ref.shape[0]
    rank = coupling_ref.shape[0] // blocks
    half = blocks // 2
    cols = cols_ref[...]
    owner = lax.rem(lax.div(cols, jnp.int32(blocks)), jnp.int32(owners))
    within = lax.rem(cols, jnp.int32(blocks))
    row = owner * half + lax.rem(within, jnp.int32(half))
    upper = lax.div(within, jnp.int32(half))
    fields = []
    for k in range(kinds):
        both = mul(pick(column(row[k:k + 1]), moments_ref.shape[0]), moments_ref[...], NN)
        both = jnp.where(column(upper[k:k + 1]) == 1, pltpu.roll(both, rank, 1), both)
        fields.append(both[:, :rank].astype(BF16))
    wide = padded(jnp.concatenate(fields, axis=1))

    def product(base):
        return mul(coupling_ref[base * rank:(base + CHUNK) * rank, :], wide, NT)

    coupled = own_columns(blocks, rank, product)
    coupled = jnp.concatenate([coupled, coupled], axis=0).T[:blocks]
    total = near_ref[...]
    step = 2 * LANES
    wide = jnp.concatenate([coupled, coupled], axis=1)
    for base in range(0, target_ref.shape[0], step):
        block = (iota(wide.shape, 1) + base) // rank
        kept = jnp.where(block == iota(wide.shape, 0), wide, 0.0).astype(BF16)
        total = total + mul(kept, target_ref[base:base + step, :], NN)
    return total


def middle_kernel(owners, cols_ref, moments_ref, coupling_ref, target_ref, near_ref, potential_ref, second_ref):
    total = potential(owners, cols_ref, moments_ref, coupling_ref, target_ref, near_ref)
    potential_ref[...] = total
    second_ref[...] = total.astype(BF16)


def last_kernel(owners, cols_ref, moments_ref, coupling_ref, target_ref, near_ref, potential_ref):
    potential_ref[...] = potential(owners, cols_ref, moments_ref, coupling_ref, target_ref, near_ref)


VMEM = pl.BlockSpec(memory_space=pltpu.VMEM)
SMEM = pl.BlockSpec(memory_space=pltpu.SMEM)
HBM = pl.BlockSpec(memory_space=pltpu.HBM)


def call(kernel, outs, *operands, specs=None, scratch=(), flops=0, moved=0):
    return pl.pallas_call(
        kernel,
        out_shape=outs,
        in_specs=specs or [VMEM] * len(operands),
        out_specs=[VMEM] * len(outs) if isinstance(outs, tuple) else VMEM,
        scratch_shapes=scratch,
        compiler_params=pltpu.CompilerParams(vmem_limit_bytes=16 << 20),
        cost_estimate=pl.CostEstimate(flops=flops, bytes_accessed=moved, transcendentals=0),
    )(*operands)


def from_behind(block, axis, distance):
    size = lax.axis_size(axis)
    return lax.ppermute(block, axis, [((i - distance) % size, i) for i in range(size)])


def shards(charges, near_vals, near_cols, source_basis, target_basis, coupling, far_cols):
    owners = lax.axis_size("cluster")
    cycle_size = lax.axis_size("blk")
    blocks, panels = charges.shape
    rank = source_basis.shape[1]
    pos = lax.axis_index("blk").reshape(1)
    near_cols = near_cols.T
    far_cols = far_cols.T
    shape = jax.ShapeDtypeStruct
    basis = shape((blocks * rank, panels), BF16)
    copies = shape((owners, blocks // 2, 2 * rank), BF16)
    field32 = shape((blocks, panels), F32)
    field16 = shape((blocks, panels), BF16)
    tile = 2 * blocks * panels * panels

    def stage(kinds):
        return [pltpu.VMEM((blocks, kinds, panels, panels), BF16), pltpu.SemaphoreType.DMA((blocks // CHUNK,))]

    def pinned(place, *arrays):
        return [pltpu.with_memory_space_constraint(array, place) for array in arrays]

    def far_exchange(copies):
        return lax.all_to_all(copies, "cluster", 0, 0, tiled=True).reshape(-1, 2 * rank)

    kept = pltpu.VMEM(basis.shape, BF16)
    kinds = near_vals.shape[1]
    rest = pltpu.VMEM((blocks, kinds - 1, panels, panels), BF16)
    near_vals, charges_hbm, source, target, coupling = pinned(
        pltpu.HBM, near_vals, charges, source_basis.reshape(basis.shape), target_basis.reshape(basis.shape), coupling)
    sent, charge, target, coupling = call(
        first_kernel, (copies, pltpu.VMEM(charges.shape, BF16), kept, kept), charges_hbm, source, target, coupling,
        specs=[HBM] * 4, scratch=[kept, pltpu.VMEM(coupling.shape, BF16), pltpu.SemaphoreType.DMA((4,))],
        flops=16 * tile, moved=2 * tile)
    target, coupling = pinned(pltpu.VMEM, target, coupling)
    order = [0]
    for distance in CHAIN:
        order = [place - distance for place in order] + order
    order = order[4:] + order[:4]
    own_scratch = stage(1) + stage(1)[1:]

    def exchange(sent, field, behind, own, vals):
        behind, sent = lax.optimization_barrier((behind, sent))
        pair = jnp.concatenate([behind, field], axis=0)
        low = jnp.concatenate([from_behind(pair, "blk", CHAIN[1]), pair], axis=0)
        high = from_behind(low, "blk", CHAIN[2])
        near = call(functools.partial(near_kernel, cycle_size, owners, order), field32,
                    pos, near_cols, low, high, *pinned(pltpu.VMEM, vals), own, specs=[SMEM] + [VMEM] * 5,
                    flops=64 * tile, moved=2 * tile)
        return far_exchange(sent), near

    own, vals = call(own_kernel, (field32, rest), charge, near_vals, specs=[VMEM, HBM], scratch=own_scratch,
                     flops=32 * tile, moved=3 * tile)
    moments, near = exchange(sent, charge, from_behind(charges, "blk", CHAIN[0]), own, vals)
    total, second = call(functools.partial(middle_kernel, owners), (pltpu.VMEM(charges.shape, F32), field16),
                         far_cols, moments, coupling, target, near, flops=48 * tile, moved=tile)
    sent = call(moments_kernel, copies, second, source, specs=[VMEM, HBM],
                scratch=[kept, pltpu.SemaphoreType.DMA(())], flops=16 * tile, moved=tile)
    own, vals, potential_one = call(
        own_store_kernel, (field32, rest, field32), second, near_vals, *pinned(pltpu.VMEM, total),
        specs=[VMEM, HBM, VMEM], scratch=own_scratch, flops=32 * tile, moved=3 * tile)
    moments, near = exchange(sent, second, from_behind(second, "blk", CHAIN[0]), own, vals)
    potential_two = call(functools.partial(last_kernel, owners), field32,
                         far_cols, moments, coupling, target, near, flops=48 * tile, moved=tile)
    return (potential_one, potential_two)


def solution(mesh):
    in_specs = (
        P(("blk", "cluster"), None),
        P(("blk", "cluster"), None, None, None),
        P(("blk", "cluster"), None),
        P(("blk", "cluster"), None, None),
        P(("blk", "cluster"), None, None),
        P(("blk", "cluster"), None, None, None),
        P(("blk", "cluster"), None),
    )
    out_specs = (P(("blk", "cluster"), None), P(("blk", "cluster"), None))
    return jax.shard_map(shards, mesh=mesh, in_specs=in_specs, out_specs=out_specs, check_vma=False)
```

```python
import functools

import jax
import jax.numpy as jnp
from jax import lax
from jax.experimental import pallas as pl
from jax.experimental.pallas import tpu as pltpu
from jax.sharding import PartitionSpec as P

F32 = jnp.float32
BF16 = jnp.bfloat16
NT = (((1,), (1,)), ((), ()))
NN = (((1,), (0,)), ((), ()))
CHUNK = 4
LANES = 128
CHAIN = (-3, 2, 1)


def mul(a, b, dims):
    return lax.dot_general(a, b, dims, preferred_element_type=F32)


def iota(shape, dim):
    return lax.broadcasted_iota(jnp.int32, shape, dim)


def pick(index, depth):
    rows = index.shape[0]
    return jnp.where(iota((rows, depth), 1) == index, 1.0, 0.0).astype(BF16)


def column(row):
    size = row.shape[1]
    square = (size, size)
    spread = jnp.broadcast_to(row.astype(F32), square)
    chosen = jnp.where(iota(square, 0) == iota(square, 1), spread, 0.0)
    return jnp.sum(chosen, axis=1, keepdims=True).astype(jnp.int32)


def padded(field):
    rows = field.shape[0]
    return jnp.concatenate([field, jnp.zeros((LANES - rows, field.shape[1]), field.dtype)], axis=0)


def own_columns(blocks, height, product):
    total = jnp.zeros((height, LANES), F32)
    lane = iota((height, LANES), 1)
    for base in range(0, blocks, CHUNK):
        result = product(base)
        for i in range(CHUNK):
            total = jnp.where(lane == base + i, result[i * height:(i + 1) * height], total)
    return total


def send_moments(field, source_ref, copies_ref):
    blocks = field.shape[0]
    rank = source_ref.shape[0] // blocks
    wide = padded(field)

    def product(base):
        return mul(source_ref[base * rank:(base + CHUNK) * rank, :], wide, NT)

    moments = own_columns(blocks, rank, product)
    moments = jnp.concatenate([moments, jnp.zeros((LANES - rank, LANES), F32)], axis=0).T
    half = blocks // 2
    packed = moments[:half] + pltpu.roll(moments[half:blocks], rank, 1)
    copies_ref[...] = jnp.broadcast_to(packed.astype(BF16)[None], copies_ref.shape)


def moments_kernel(field_ref, source_ref, copies_ref):
    send_moments(field_ref[...], source_ref, copies_ref)


def first_kernel(charge_hbm, source_hbm, target_hbm, coupling_hbm,
                 copies_ref, charge_ref, target_ref, packed_ref, source_ref, coupling_ref, sems):
    pairs = [(charge_hbm, charge_ref), (source_hbm, source_ref), (coupling_hbm, coupling_ref), (target_hbm, target_ref)]
    moves = [pltpu.make_async_copy(a, b, sems.at[n]) for n, (a, b) in enumerate(pairs)]
    for move in moves:
        move.start()
    moves[0].wait()
    moves[1].wait()
    send_moments(charge_ref[...], source_ref, copies_ref)
    moves[2].wait()
    blocks, kinds, rank, _ = coupling_ref.shape
    for i in range(blocks):
        packed_ref[i * rank:(i + 1) * rank, :] = jnp.concatenate([coupling_ref[i, k] for k in range(kinds)], axis=1)
    moves[3].wait()


def fetch(source, dest, sems):
    moves = []
    for n in range(dest.shape[0] // CHUNK):
        part = pl.ds(n * CHUNK, CHUNK)
        moves.append(pltpu.make_async_copy(source.at[part], dest.at[part], sems.at[n]))
    for move in moves:
        move.start()
    return moves


def near_product(fields, vals_ref):
    blocks, panels = fields[0].shape
    wide = padded(jnp.concatenate(fields, axis=1))

    def product(base):
        vals = [vals_ref[base:base + CHUNK, k].reshape(CHUNK * panels, panels) for k in range(len(fields))]
        return mul(jnp.concatenate(vals, axis=1), wide, NT)

    return own_columns(blocks, panels, product).T[:blocks]


def own_kernel(field_ref, vals_hbm, near_ref, rest_ref, vals_ref, sems, rest_sems):
    moves = fetch(vals_hbm.at[:, pl.ds(0, 1)], vals_ref, sems)
    rest = fetch(vals_hbm.at[:, pl.ds(1, rest_ref.shape[1])], rest_ref, rest_sems)
    for move in moves:
        move.wait()
    near_ref[...] = near_product([field_ref[...]], vals_ref)
    for move in rest:
        move.wait()


def own_store_kernel(field_ref, vals_hbm, kept_ref, near_ref, rest_ref, stored_ref, vals_ref, sems, rest_sems):
    stored_ref[...] = kept_ref[...]
    own_kernel(field_ref, vals_hbm, near_ref, rest_ref, vals_ref, sems, rest_sems)


def near_kernel(cycle_size, owners, order, pos_ref, cols_ref, low_ref, high_ref, vals_ref, own_ref, near_ref):
    blocks = own_ref.shape[0]
    kinds = cols_ref.shape[0]
    cols = cols_ref[...]
    target = lax.div(cols, jnp.int32(blocks * owners))
    offset = lax.rem(target - pos_ref[0] + cycle_size, jnp.int32(cycle_size))
    slot = jnp.zeros(cols.shape, jnp.int32)
    for place in range(len(order) - 1, -1, -1):
        slot = jnp.where(offset == order[place] % cycle_size, place, slot)
    row = slot * blocks + lax.rem(cols, jnp.int32(blocks))
    span = low_ref.shape[0]
    fields = []
    for k in range(1, kinds):
        index = column(row[k:k + 1])
        field = mul(pick(index, span), low_ref[...], NN)
        field = field + mul(pick(index - span, span), high_ref[...], NN)
        fields.append(field.astype(BF16))
    near_ref[...] = own_ref[...] + near_product(fields, vals_ref)


def potential(owners, cols_ref, moments_ref, coupling_ref, target_ref, near_ref):
    blocks, panels = near_ref.shape
    kinds = cols_ref.shape[0]
    rank = coupling_ref.shape[0] // blocks
    half = blocks // 2
    cols = cols_ref[...]
    owner = lax.rem(lax.div(cols, jnp.int32(blocks)), jnp.int32(owners))
    within = lax.rem(cols, jnp.int32(blocks))
    row = owner * half + lax.rem(within, jnp.int32(half))
    upper = lax.div(within, jnp.int32(half))
    fields = []
    for k in range(kinds):
        both = mul(pick(column(row[k:k + 1]), moments_ref.shape[0]), moments_ref[...], NN)
        both = jnp.where(column(upper[k:k + 1]) == 1, pltpu.roll(both, rank, 1), both)
        fields.append(both[:, :rank].astype(BF16))
    wide = padded(jnp.concatenate(fields, axis=1))

    def product(base):
        return mul(coupling_ref[base * rank:(base + CHUNK) * rank, :], wide, NT)

    coupled = own_columns(blocks, rank, product)
    coupled = jnp.concatenate([coupled, coupled], axis=0).T[:blocks]
    total = near_ref[...]
    step = 2 * LANES
    wide = jnp.concatenate([coupled, coupled], axis=1)
    for base in range(0, target_ref.shape[0], step):
        block = (iota(wide.shape, 1) + base) // rank
        kept = jnp.where(block == iota(wide.shape, 0), wide, 0.0).astype(BF16)
        total = total + mul(kept, target_ref[base:base + step, :], NN)
    return total


def middle_kernel(owners, cols_ref, moments_ref, coupling_ref, target_ref, near_ref, source_hbm,
                  potential_ref, second_ref, source_ref, sem):
    move = pltpu.make_async_copy(source_hbm, source_ref, sem)
    move.start()
    total = potential(owners, cols_ref, moments_ref, coupling_ref, target_ref, near_ref)
    potential_ref[...] = total
    second_ref[...] = total.astype(BF16)
    move.wait()


def last_kernel(owners, cols_ref, moments_ref, coupling_ref, target_ref, near_ref, potential_ref):
    potential_ref[...] = potential(owners, cols_ref, moments_ref, coupling_ref, target_ref, near_ref)


VMEM = pl.BlockSpec(memory_space=pltpu.VMEM)
SMEM = pl.BlockSpec(memory_space=pltpu.SMEM)
HBM = pl.BlockSpec(memory_space=pltpu.HBM)


def call(kernel, outs, *operands, specs=None, scratch=(), flops=0, moved=0):
    return pl.pallas_call(
        kernel,
        out_shape=outs,
        in_specs=specs or [VMEM] * len(operands),
        out_specs=[VMEM] * len(outs) if isinstance(outs, tuple) else VMEM,
        scratch_shapes=scratch,
        compiler_params=pltpu.CompilerParams(vmem_limit_bytes=16 << 20),
        cost_estimate=pl.CostEstimate(flops=flops, bytes_accessed=moved, transcendentals=0),
    )(*operands)


def from_behind(block, axis, distance):
    size = lax.axis_size(axis)
    return lax.ppermute(block, axis, [((i - distance) % size, i) for i in range(size)])


def shards(charges, near_vals, near_cols, source_basis, target_basis, coupling, far_cols):
    owners = lax.axis_size("cluster")
    cycle_size = lax.axis_size("blk")
    blocks, panels = charges.shape
    rank = source_basis.shape[1]
    pos = lax.axis_index("blk").reshape(1)
    near_cols = near_cols.T
    far_cols = far_cols.T
    shape = jax.ShapeDtypeStruct
    basis = shape((blocks * rank, panels), BF16)
    copies = shape((owners, blocks // 2, 2 * rank), BF16)
    field32 = shape((blocks, panels), F32)
    field16 = shape((blocks, panels), BF16)
    tile = 2 * blocks * panels * panels

    def stage(kinds):
        return [pltpu.VMEM((blocks, kinds, panels, panels), BF16), pltpu.SemaphoreType.DMA((blocks // CHUNK,))]

    def pinned(place, *arrays):
        return [pltpu.with_memory_space_constraint(array, place) for array in arrays]

    def far_exchange(copies):
        return lax.all_to_all(copies, "cluster", 0, 0, tiled=True).reshape(-1, 2 * rank)

    kept = pltpu.VMEM(basis.shape, BF16)
    kinds = near_vals.shape[1]
    rest = pltpu.VMEM((blocks, kinds - 1, panels, panels), BF16)
    near_vals, charges_hbm, source, target, coupling = pinned(
        pltpu.HBM, near_vals, charges, source_basis.reshape(basis.shape), target_basis.reshape(basis.shape), coupling)
    sent, charge, target, coupling = call(
        first_kernel, (copies, pltpu.VMEM(charges.shape, BF16), kept, kept), charges_hbm, source, target, coupling,
        specs=[HBM] * 4, scratch=[kept, pltpu.VMEM(coupling.shape, BF16), pltpu.SemaphoreType.DMA((4,))],
        flops=16 * tile, moved=2 * tile)
    target, coupling = pinned(pltpu.VMEM, target, coupling)
    order = [0]
    for distance in CHAIN:
        order = [place - distance for place in order] + order
    order = order[4:] + order[:4]
    own_scratch = stage(1) + stage(1)[1:]

    def exchange(sent, field, behind, own, vals):
        behind, sent = lax.optimization_barrier((behind, sent))
        pair = jnp.concatenate([behind, field], axis=0)
        low = jnp.concatenate([from_behind(pair, "blk", CHAIN[1]), pair], axis=0)
        high = from_behind(low, "blk", CHAIN[2])
        near = call(functools.partial(near_kernel, cycle_size, owners, order), field32,
                    pos, near_cols, low, high, *pinned(pltpu.VMEM, vals), own, specs=[SMEM] + [VMEM] * 5,
                    flops=64 * tile, moved=2 * tile)
        return far_exchange(sent), near

    own, vals = call(own_kernel, (field32, rest), charge, near_vals, specs=[VMEM, HBM], scratch=own_scratch,
                     flops=32 * tile, moved=3 * tile)
    moments, near = exchange(sent, charge, from_behind(charges, "blk", CHAIN[0]), own, vals)
    total, second, source = call(
        functools.partial(middle_kernel, owners), (pltpu.VMEM(charges.shape, F32), field16, kept),
        far_cols, moments, coupling, target, near, source, specs=[VMEM] * 5 + [HBM],
        scratch=[pltpu.SemaphoreType.DMA(())], flops=48 * tile, moved=tile)
    sent = call(moments_kernel, copies, second, *pinned(pltpu.VMEM, source), flops=16 * tile, moved=tile)
    own, vals, potential_one = call(
        own_store_kernel, (field32, rest, field32), second, near_vals, *pinned(pltpu.VMEM, total),
        specs=[VMEM, HBM, VMEM], scratch=own_scratch, flops=32 * tile, moved=3 * tile)
    moments, near = exchange(sent, second, from_behind(second, "blk", CHAIN[0]), own, vals)
    potential_two = call(functools.partial(last_kernel, owners), field32,
                         far_cols, moments, coupling, target, near, flops=48 * tile, moved=tile)
    return (potential_one, potential_two)


def solution(mesh):
    in_specs = (
        P(("blk", "cluster"), None),
        P(("blk", "cluster"), None, None, None),
        P(("blk", "cluster"), None),
        P(("blk", "cluster"), None, None),
        P(("blk", "cluster"), None, None),
        P(("blk", "cluster"), None, None, None),
        P(("blk", "cluster"), None),
    )
    out_specs = (P(("blk", "cluster"), None), P(("blk", "cluster"), None))
    return jax.shard_map(shards, mesh=mesh, in_specs=in_specs, out_specs=out_specs, check_vma=False)
```

```python
import functools

import jax
import jax.numpy as jnp
from jax import lax
from jax.experimental import pallas as pl
from jax.experimental.pallas import tpu as pltpu
from jax.sharding import PartitionSpec as P

F32 = jnp.float32
BF16 = jnp.bfloat16
NT = (((1,), (1,)), ((), ()))
NN = (((1,), (0,)), ((), ()))
CHUNK = 4
LANES = 128
CHAIN = (2, -3, 1)


def mul(a, b, dims):
    return lax.dot_general(a, b, dims, preferred_element_type=F32)


def iota(shape, dim):
    return lax.broadcasted_iota(jnp.int32, shape, dim)


def pick(index, depth):
    rows = index.shape[0]
    return jnp.where(iota((rows, depth), 1) == index, 1.0, 0.0).astype(BF16)


def column(row):
    size = row.shape[1]
    square = (size, size)
    spread = jnp.broadcast_to(row.astype(F32), square)
    chosen = jnp.where(iota(square, 0) == iota(square, 1), spread, 0.0)
    return jnp.sum(chosen, axis=1, keepdims=True).astype(jnp.int32)


def padded(field):
    rows = field.shape[0]
    return jnp.concatenate([field, jnp.zeros((LANES - rows, field.shape[1]), field.dtype)], axis=0)


def own_columns(blocks, height, product):
    total = jnp.zeros((height, LANES), F32)
    lane = iota((height, LANES), 1)
    for base in range(0, blocks, CHUNK):
        result = product(base)
        for i in range(CHUNK):
            total = jnp.where(lane == base + i, result[i * height:(i + 1) * height], total)
    return total


def send_moments(field, source_ref, copies_ref):
    blocks = field.shape[0]
    rank = source_ref.shape[0] // blocks
    wide = padded(field)

    def product(base):
        return mul(source_ref[base * rank:(base + CHUNK) * rank, :], wide, NT)

    moments = own_columns(blocks, rank, product)
    moments = jnp.concatenate([moments, jnp.zeros((LANES - rank, LANES), F32)], axis=0).T
    half = blocks // 2
    packed = moments[:half] + pltpu.roll(moments[half:blocks], rank, 1)
    copies_ref[...] = jnp.broadcast_to(packed.astype(BF16)[None], copies_ref.shape)


def moments_kernel(field_ref, source_hbm, copies_ref, source_ref, sem):
    move = pltpu.make_async_copy(source_hbm, source_ref, sem)
    move.start()
    move.wait()
    send_moments(field_ref[...], source_ref, copies_ref)


def first_kernel(charge_hbm, source_hbm, target_hbm, coupling_hbm,
                 copies_ref, charge_ref, target_ref, packed_ref, source_ref, coupling_ref, sems):
    pairs = [(charge_hbm, charge_ref), (source_hbm, source_ref), (coupling_hbm, coupling_ref), (target_hbm, target_ref)]
    moves = [pltpu.make_async_copy(a, b, sems.at[n]) for n, (a, b) in enumerate(pairs)]
    for move in moves:
        move.start()
    moves[0].wait()
    moves[1].wait()
    send_moments(charge_ref[...], source_ref, copies_ref)
    moves[2].wait()
    blocks, kinds, rank, _ = coupling_ref.shape
    for i in range(blocks):
        packed_ref[i * rank:(i + 1) * rank, :] = jnp.concatenate([coupling_ref[i, k] for k in range(kinds)], axis=1)
    moves[3].wait()


def fetch(source, dest, sems):
    moves = []
    for n in range(dest.shape[0] // CHUNK):
        part = pl.ds(n * CHUNK, CHUNK)
        moves.append(pltpu.make_async_copy(source.at[part], dest.at[part], sems.at[n]))
    for move in moves:
        move.start()
    return moves


def near_product(fields, vals_ref):
    blocks, panels = fields[0].shape
    wide = padded(jnp.concatenate(fields, axis=1))

    def product(base):
        vals = [vals_ref[base:base + CHUNK, k].reshape(CHUNK * panels, panels) for k in range(len(fields))]
        return mul(jnp.concatenate(vals, axis=1), wide, NT)

    return own_columns(blocks, panels, product).T[:blocks]


def own_kernel(field_ref, vals_hbm, near_ref, rest_ref, vals_ref, sems, rest_sems):
    moves = fetch(vals_hbm.at[:, pl.ds(0, 1)], vals_ref, sems)
    rest = fetch(vals_hbm.at[:, pl.ds(1, rest_ref.shape[1])], rest_ref, rest_sems)
    for move in moves:
        move.wait()
    near_ref[...] = near_product([field_ref[...]], vals_ref)
    for move in rest:
        move.wait()


def own_store_kernel(field_ref, vals_hbm, kept_ref, near_ref, rest_ref, stored_ref, vals_ref, sems, rest_sems):
    stored_ref[...] = kept_ref[...]
    own_kernel(field_ref, vals_hbm, near_ref, rest_ref, vals_ref, sems, rest_sems)


def near_kernel(cycle_size, owners, order, pos_ref, cols_ref, low_ref, high_ref, vals_ref, own_ref, near_ref):
    blocks = own_ref.shape[0]
    kinds = cols_ref.shape[0]
    cols = cols_ref[...]
    target = lax.div(cols, jnp.int32(blocks * owners))
    offset = lax.rem(target - pos_ref[0] + cycle_size, jnp.int32(cycle_size))
    slot = jnp.zeros(cols.shape, jnp.int32)
    for place in range(len(order) - 1, -1, -1):
        slot = jnp.where(offset == order[place] % cycle_size, place, slot)
    row = slot * blocks + lax.rem(cols, jnp.int32(blocks))
    span = low_ref.shape[0]
    fields = []
    for k in range(1, kinds):
        index = column(row[k:k + 1])
        field = mul(pick(index, span), low_ref[...], NN)
        field = field + mul(pick(index - span, span), high_ref[...], NN)
        fields.append(field.astype(BF16))
    near_ref[...] = own_ref[...] + near_product(fields, vals_ref)


def potential(owners, cols_ref, moments_ref, coupling_ref, target_ref, near_ref):
    blocks, panels = near_ref.shape
    kinds = cols_ref.shape[0]
    rank = coupling_ref.shape[0] // blocks
    half = blocks // 2
    cols = cols_ref[...]
    owner = lax.rem(lax.div(cols, jnp.int32(blocks)), jnp.int32(owners))
    within = lax.rem(cols, jnp.int32(blocks))
    row = owner * half + lax.rem(within, jnp.int32(half))
    upper = lax.div(within, jnp.int32(half))
    fields = []
    for k in range(kinds):
        both = mul(pick(column(row[k:k + 1]), moments_ref.shape[0]), moments_ref[...], NN)
        both = jnp.where(column(upper[k:k + 1]) == 1, pltpu.roll(both, rank, 1), both)
        fields.append(both[:, :rank].astype(BF16))
    wide = padded(jnp.concatenate(fields, axis=1))

    def product(base):
        return mul(coupling_ref[base * rank:(base + CHUNK) * rank, :], wide, NT)

    coupled = own_columns(blocks, rank, product)
    coupled = jnp.concatenate([coupled, coupled], axis=0).T[:blocks]
    total = near_ref[...]
    step = 2 * LANES
    wide = jnp.concatenate([coupled, coupled], axis=1)
    for base in range(0, target_ref.shape[0], step):
        block = (iota(wide.shape, 1) + base) // rank
        kept = jnp.where(block == iota(wide.shape, 0), wide, 0.0).astype(BF16)
        total = total + mul(kept, target_ref[base:base + step, :], NN)
    return total


def middle_kernel(owners, cols_ref, moments_ref, coupling_ref, target_ref, near_ref, potential_ref, second_ref):
    total = potential(owners, cols_ref, moments_ref, coupling_ref, target_ref, near_ref)
    potential_ref[...] = total
    second_ref[...] = total.astype(BF16)


def last_kernel(owners, cols_ref, moments_ref, coupling_ref, target_ref, near_ref, potential_ref):
    potential_ref[...] = potential(owners, cols_ref, moments_ref, coupling_ref, target_ref, near_ref)


VMEM = pl.BlockSpec(memory_space=pltpu.VMEM)
SMEM = pl.BlockSpec(memory_space=pltpu.SMEM)
HBM = pl.BlockSpec(memory_space=pltpu.HBM)


def call(kernel, outs, *operands, specs=None, scratch=(), flops=0, moved=0):
    return pl.pallas_call(
        kernel,
        out_shape=outs,
        in_specs=specs or [VMEM] * len(operands),
        out_specs=[VMEM] * len(outs) if isinstance(outs, tuple) else VMEM,
        scratch_shapes=scratch,
        compiler_params=pltpu.CompilerParams(vmem_limit_bytes=16 << 20),
        cost_estimate=pl.CostEstimate(flops=flops, bytes_accessed=moved, transcendentals=0),
    )(*operands)


def from_behind(block, axis, distance):
    size = lax.axis_size(axis)
    return lax.ppermute(block, axis, [((i - distance) % size, i) for i in range(size)])


def shards(charges, near_vals, near_cols, source_basis, target_basis, coupling, far_cols):
    owners = lax.axis_size("cluster")
    cycle_size = lax.axis_size("blk")
    blocks, panels = charges.shape
    rank = source_basis.shape[1]
    pos = lax.axis_index("blk").reshape(1)
    near_cols = near_cols.T
    far_cols = far_cols.T
    shape = jax.ShapeDtypeStruct
    basis = shape((blocks * rank, panels), BF16)
    copies = shape((owners, blocks // 2, 2 * rank), BF16)
    field32 = shape((blocks, panels), F32)
    field16 = shape((blocks, panels), BF16)
    tile = 2 * blocks * panels * panels

    def stage(kinds):
        return [pltpu.VMEM((blocks, kinds, panels, panels), BF16), pltpu.SemaphoreType.DMA((blocks // CHUNK,))]

    def pinned(place, *arrays):
        return [pltpu.with_memory_space_constraint(array, place) for array in arrays]

    def far_exchange(copies):
        return lax.all_to_all(copies, "cluster", 0, 0, tiled=True).reshape(-1, 2 * rank)

    kept = pltpu.VMEM(basis.shape, BF16)
    kinds = near_vals.shape[1]
    rest = pltpu.VMEM((blocks, kinds - 1, panels, panels), BF16)
    near_vals, charges_hbm, source, target, coupling = pinned(
        pltpu.HBM, near_vals, charges, source_basis.reshape(basis.shape), target_basis.reshape(basis.shape), coupling)
    sent, charge, target, coupling = call(
        first_kernel, (copies, pltpu.VMEM(charges.shape, BF16), kept, kept), charges_hbm, source, target, coupling,
        specs=[HBM] * 4, scratch=[kept, pltpu.VMEM(coupling.shape, BF16), pltpu.SemaphoreType.DMA((4,))],
        flops=16 * tile, moved=2 * tile)
    target, coupling = pinned(pltpu.VMEM, target, coupling)
    order = [0]
    for distance in CHAIN:
        order = [place - distance for place in order] + order
    order = order[4:] + order[:4]
    own_scratch = stage(1) + stage(1)[1:]

    def exchange(sent, field, behind, own, vals):
        behind, sent = lax.optimization_barrier((behind, sent))
        pair = jnp.concatenate([behind, field], axis=0)
        low = jnp.concatenate([from_behind(pair, "blk", CHAIN[1]), pair], axis=0)
        high = from_behind(low, "blk", CHAIN[2])
        near = call(functools.partial(near_kernel, cycle_size, owners, order), field32,
                    pos, near_cols, low, high, *pinned(pltpu.VMEM, vals), own, specs=[SMEM] + [VMEM] * 5,
                    flops=64 * tile, moved=2 * tile)
        return far_exchange(sent), near

    own, vals = call(own_kernel, (field32, rest), charge, near_vals, specs=[VMEM, HBM], scratch=own_scratch,
                     flops=32 * tile, moved=3 * tile)
    moments, near = exchange(sent, charge, from_behind(charges, "blk", CHAIN[0]), own, vals)
    total, second = call(functools.partial(middle_kernel, owners), (pltpu.VMEM(charges.shape, F32), field16),
                         far_cols, moments, coupling, target, near, flops=48 * tile, moved=tile)
    sent = call(moments_kernel, copies, second, source, specs=[VMEM, HBM],
                scratch=[kept, pltpu.SemaphoreType.DMA(())], flops=16 * tile, moved=tile)
    own, vals, potential_one = call(
        own_store_kernel, (field32, rest, field32), second, near_vals, *pinned(pltpu.VMEM, total),
        specs=[VMEM, HBM, VMEM], scratch=own_scratch, flops=32 * tile, moved=3 * tile)
    moments, near = exchange(sent, second, from_behind(second, "blk", CHAIN[0]), own, vals)
    potential_two = call(functools.partial(last_kernel, owners), field32,
                         far_cols, moments, coupling, target, near, flops=48 * tile, moved=tile)
    return (potential_one, potential_two)


def solution(mesh):
    in_specs = (
        P(("blk", "cluster"), None),
        P(("blk", "cluster"), None, None, None),
        P(("blk", "cluster"), None),
        P(("blk", "cluster"), None, None),
        P(("blk", "cluster"), None, None),
        P(("blk", "cluster"), None, None, None),
        P(("blk", "cluster"), None),
    )
    out_specs = (P(("blk", "cluster"), None), P(("blk", "cluster"), None))
    return jax.shard_map(shards, mesh=mesh, in_specs=in_specs, out_specs=out_specs, check_vma=False)
```
